512 devices in a mesh: section: 16 (over x, y_lo, core), dp: 32 (over z, y_hi).
Axes of the slice: x: 4, y: 8 (y_hi: 4, y_lo: 2; y = y_hi * 2 + y_lo), z: 8, core: 2. Of those that a mesh axis runs over, the one named last changes fastest.
Arguments:
- feedforward_entry_states: bfloat16 [16, 512, 32, 1152], P('section', 'dp'), may hold values from -6 to 6
- stored_hidden_preacts: bfloat16 [16, 512, 32, 2176], P('section', 'dp'), may hold values from -6 to 6
- layernorm_multiplier: float32 [16, 1152], P('section'), may hold values from 0.1 to 1.9
- expanding_projector: bfloat16 [16, 1152, 2176], P('section', 'dp'), may hold values from -0.1875 to 0.1875
- contracting_projector: bfloat16 [16, 2176, 1152], P('section', 'dp'), may hold values from -0.125 to 0.125
- caption_tower_outputs: bfloat16 [16, 512, 1152], P('section', 'dp'), may hold values from -6 to 6
- similarity_sharpness: float32 [1], replicated, may hold values from 4 to 12
- similarity_shift_term: float32 [1], replicated, may hold values from -3 to -1
- objective_upstream_grad: float32 [1], replicated, may hold values from 8 to 48
Outputs:
- prev_grad: bfloat16 [16, 512, 32, 1152], P('section', 'dp')
- text_grad: bfloat16 [16, 512, 1152], P('section', 'dp')
The draws below stay inside these ranges and needn't reach their ends.
All inputs are finite; a program needn't handle non-finite values.
Results may differ from the reference program's by a relative error of at most 0.013.
Values may be sent and summed in bfloat16 or wider, within the bound.
No kernel may reach another device: no remote copies, remote signals or barrier semaphores. Data moves between devices by JAX's collectives and lax.ppermute only.
A program may use at most 128 MiB of HBM per device.

```python
import math
import jax
import jax.numpy as jnp
from jax import lax

D = 1152
FF = 2176
PATCHES = 32
IMGS = 512
MICRO = 16


def shared_classes(key):
    class_ids = jax.random.randint(jax.random.fold_in(key, 101), (MICRO, IMGS), 0, 8)
    class_table = jax.random.normal(jax.random.fold_in(key, 102), (MICRO, 8, D), jnp.float32)
    return jnp.take_along_axis(class_table, class_ids[:, :, None], axis=1)


def draw_feedforward_entry_states(key, part):
    class_rows = shared_classes(key)
    key = jax.random.fold_in(key, 3)
    strength = jax.random.uniform(jax.random.fold_in(key, 1), (MICRO, IMGS, 1, 1), jnp.float32, 0.15, 0.35)
    own_rows = jax.random.normal(jax.random.fold_in(key, 2), (MICRO, IMGS, 1, D), jnp.float32)
    patch_noise = jax.random.normal(jax.random.fold_in(key, 4), (MICRO, IMGS, PATCHES, D), jnp.float32)
    values = strength * class_rows[:, :, None, :] + 0.12 * own_rows + 0.9 * patch_noise
    return jnp.clip(values, -6.0, 6.0).astype(jnp.bfloat16)


def draw_caption_tower_outputs(key, part):
    class_rows = shared_classes(key)
    key = jax.random.fold_in(key, 5)
    strength = jax.random.uniform(jax.random.fold_in(key, 1), (MICRO, IMGS, 1), jnp.float32, 0.5, 1.0)
    text_noise = jax.random.normal(jax.random.fold_in(key, 2), (MICRO, IMGS, D), jnp.float32)
    values = strength * class_rows + 0.8 * text_noise
    return jnp.clip(values, -6.0, 6.0).astype(jnp.bfloat16)


def block_levels(own_key, shape, shards, low, largest):
    def one(dim, blocks):
        steps = jax.random.uniform(jax.random.fold_in(jax.random.fold_in(own_key, 6), dim), (blocks,), jnp.float32, low / len(shards), largest / len(shards))
        return jnp.repeat(jnp.exp(steps), shape[dim] // blocks).reshape((-1,) + (1,) * (len(shape) - dim - 1))

    level = one(*shards[0])
    for cut in shards[1:]:
        level = level * one(*cut)
    return level


def centred(stream_key, dims, scale, most, split=(), held_as=jnp.bfloat16):
    level = block_levels(stream_key, dims, split, -0.22, 0.18) if split else 1.0
    result = jax.random.normal(stream_key, dims, jnp.float32) * scale * level
    return jnp.minimum(jnp.maximum(result, -most), most).astype(held_as)


def setup_inputs(seed: int = 0) -> dict:
    arg_keys = jax.random.split(jax.random.key(seed), 10)
    return {
        "feedforward_entry_states": draw_feedforward_entry_states(jax.random.fold_in(arg_keys[9], 71), 0),
        "stored_hidden_preacts": centred(arg_keys[1], (MICRO, IMGS, PATCHES, FF), 1.0, 6.0, ((0, 16), (1, 32))),
        "layernorm_multiplier": jnp.clip(1.0 + 0.18 * jax.random.normal(arg_keys[2], (MICRO, D), jnp.float32), 0.1, 1.9),
        "expanding_projector": centred(arg_keys[3], (MICRO, D, FF), D ** -0.5, 0.1875, ((0, 16), (1, 32))),
        "contracting_projector": centred(arg_keys[4], (MICRO, FF, D), FF ** -0.5, 0.125, ((0, 16), (1, 32))),
        "caption_tower_outputs": draw_caption_tower_outputs(jax.random.fold_in(arg_keys[9], 71), 0),
        "similarity_sharpness": jnp.clip(jnp.exp(jax.random.uniform(arg_keys[6], (1,), jnp.float32, math.log(4.0), math.log(12.0))), 4.0, 12.0),
        "similarity_shift_term": jnp.clip(jax.random.uniform(arg_keys[7], (1,), jnp.float32, -3.0, -1.0), -3.0, -1.0),
        "objective_upstream_grad": jnp.clip(jnp.exp(jax.random.uniform(arg_keys[8], (1,), jnp.float32, math.log(8.0), math.log(48.0))), 8.0, 48.0),
    }


EPSILON = 1e-06
TANH_SCALE = 0.7978845608028654
CUBIC_TERM = 0.044715

def gelu_slope(preact):
    inner = TANH_SCALE * (preact + CUBIC_TERM * preact * preact * preact)
    tangent = jnp.tanh(inner)
    return 0.5 * (1.0 + tangent) + 0.5 * preact * (1.0 - tangent * tangent) * TANH_SCALE * (1.0 + 3.0 * CUBIC_TERM * preact * preact)

def unit_rows(values):
    inverse = lax.rsqrt(lax.optimization_barrier(jnp.sum(values * values, axis=-1, keepdims=True)) + EPSILON)
    return (values * inverse, inverse)

def pairwise_weight(image_normalized, text_normalized, image_index, text_index, smoothing_coefficient, logit_offset, weight_factor):
    pair_logits = smoothing_coefficient * lax.dot_general(image_normalized, text_normalized, (((1,), (1,)), ((), ())), preferred_element_type=jnp.float32) + logit_offset
    signs = jnp.where(image_index[:, None] == text_index[None, :], 1.0, -1.0).astype(jnp.float32)
    return (weight_factor * -signs * jax.nn.sigmoid(-signs * pair_logits)).astype(jnp.bfloat16)

def norm_backward(tokens, normed_grad, layernorm_multiplier):
    centered = tokens - lax.optimization_barrier(jnp.mean(tokens, axis=-1, keepdims=True))
    inverse = lax.rsqrt(lax.optimization_barrier(jnp.mean(centered * centered, axis=-1, keepdims=True)) + EPSILON)
    normal = centered * inverse
    scaled = normed_grad * layernorm_multiplier
    return inverse * (scaled - lax.optimization_barrier(jnp.mean(scaled, axis=-1, keepdims=True)) - normal * lax.optimization_barrier(jnp.mean(scaled * normal, axis=-1, keepdims=True)))

def single_batch(operand_list, smoothing_coefficient, logit_offset, weight_factor):
    feedforward_entry_states, stored_hidden_preacts, layernorm_multiplier, expanding_projector, contracting_projector, caption_tower_outputs = operand_list
    images, patches, model_width = feedforward_entry_states.shape
    hidden = stored_hidden_preacts.shape[-1]
    tokens = feedforward_entry_states.reshape(images * patches, model_width).astype(jnp.float32)
    preact = stored_hidden_preacts.reshape(images * patches, hidden).astype(jnp.float32)
    activated = jax.nn.gelu(preact, approximate=True).astype(jnp.bfloat16)
    mlp_out = jnp.dot(activated, contracting_projector, preferred_element_type=jnp.float32)
    pooled = lax.optimization_barrier(jnp.mean((tokens + mlp_out).reshape(images, patches, model_width), axis=1))
    image_dir, image_inverse = unit_rows(pooled)
    image_normalized = image_dir.astype(jnp.bfloat16)
    text_dir, text_inverse = unit_rows(caption_tower_outputs.astype(jnp.float32))
    text_normalized = text_dir.astype(jnp.bfloat16)
    identity_matrix = lax.iota(jnp.int32, images)
    weight_array = pairwise_weight(image_normalized, text_normalized, identity_matrix, identity_matrix, smoothing_coefficient, logit_offset, weight_factor)
    image_sum = jnp.dot(weight_array, text_normalized, preferred_element_type=jnp.float32)
    text_sum = lax.dot_general(weight_array, image_normalized, (((0,), (0,)), ((), ())), preferred_element_type=jnp.float32)
    text_grad = ((text_sum - text_dir * lax.optimization_barrier(jnp.sum(text_dir * text_sum, axis=-1, keepdims=True))) * text_inverse).astype(jnp.bfloat16)
    pooled_grad = (image_sum - image_dir * lax.optimization_barrier(jnp.sum(image_dir * image_sum, axis=-1, keepdims=True))) * image_inverse
    share = pooled_grad / patches
    token_grad = share.astype(jnp.bfloat16)
    hidden_grad = lax.dot_general(token_grad, contracting_projector, (((1,), (1,)), ((), ())), preferred_element_type=jnp.float32)
    slope = gelu_slope(preact).reshape(images, patches, hidden)
    preact_grad = (hidden_grad[:, None, :] * slope).astype(jnp.bfloat16).reshape(images * patches, hidden)
    normed_grad = lax.dot_general(preact_grad, expanding_projector, (((1,), (1,)), ((), ())), preferred_element_type=jnp.float32)
    inner_grad = norm_backward(tokens, normed_grad, layernorm_multiplier).reshape(images, patches, model_width)
    span_grad = (share[:, None, :] + inner_grad).astype(jnp.bfloat16)
    return (span_grad, text_grad)

def reference(feedforward_entry_states, stored_hidden_preacts, layernorm_multiplier, expanding_projector, contracting_projector, caption_tower_outputs, similarity_sharpness, similarity_shift_term, objective_upstream_grad):
    smoothing_coefficient = similarity_sharpness[0]
    logit_offset = similarity_shift_term[0]
    weight_factor = objective_upstream_grad[0] * smoothing_coefficient

    def run_batch(operand_list):
        return single_batch(operand_list, smoothing_coefficient, logit_offset, weight_factor)
    span_grad, text_grad = lax.map(run_batch, (feedforward_entry_states, stored_hidden_preacts, layernorm_multiplier, expanding_projector, contracting_projector, caption_tower_outputs))
    return (jnp.roll(span_grad, -1, axis=0), text_grad)
```

```python
import jax
import jax.numpy as jnp
from jax import lax
from jax.sharding import Mesh, PartitionSpec as P

EPSILON = 1e-06
TANH_SCALE = 0.7978845608028654
CUBIC_TERM = 0.044715
Y_SHARDS = 4


def from_ahead(array, axis, by):
    peers = lax.axis_size(axis)
    return lax.ppermute(array, axis, [((i + by) % peers, i) for i in range(peers)])


def gelu_slope(preact):
    inner = TANH_SCALE * (preact + CUBIC_TERM * preact * preact * preact)
    tangent = jnp.tanh(inner)
    return 0.5 * (1.0 + tangent) + 0.5 * preact * (1.0 - tangent * tangent) * TANH_SCALE * (
        1.0 + 3.0 * CUBIC_TERM * preact * preact
    )


def unit_rows(values):
    inverse = lax.rsqrt(jnp.sum(values * values, axis=-1, keepdims=True) + EPSILON)
    return (values * inverse, inverse)


def pair_weights(image_unit, text_unit, image_index, text_index, sharpness, shift, factor):
    logits = (
        sharpness
        * lax.dot_general(
            image_unit, text_unit, (((1,), (1,)), ((), ())), preferred_element_type=jnp.float32
        )
        + shift
    )
    signs = jnp.where(image_index[:, None] == text_index[None, :], 1.0, -1.0).astype(jnp.float32)
    return (factor * -signs * jax.nn.sigmoid(-signs * logits)).astype(jnp.bfloat16)


def norm_backward(tokens, normed_grad, layernorm_multiplier):
    centered = tokens - jnp.mean(tokens, axis=-1, keepdims=True)
    inverse = lax.rsqrt(jnp.mean(centered * centered, axis=-1, keepdims=True) + EPSILON)
    normal = centered * inverse
    scaled = normed_grad * layernorm_multiplier
    return inverse * (
        scaled
        - jnp.mean(scaled, axis=-1, keepdims=True)
        - normal * jnp.mean(scaled * normal, axis=-1, keepdims=True)
    )


def exchange_z(blocks):
    return lax.all_to_all(blocks, "z", 0, 0)


def gather_y(shard, y):
    ahead = [shard] + [from_ahead(shard, "y", k) for k in range(1, Y_SHARDS)]
    placed = [
        lax.select_n(y, *[ahead[(a - own) % Y_SHARDS] for own in range(Y_SHARDS)])
        for a in range(Y_SHARDS)
    ]
    return jnp.concatenate(placed, axis=0)


def per_device(
    feedforward_entry_states,
    stored_hidden_preacts,
    layernorm_multiplier,
    expanding_projector,
    contracting_projector,
    caption_tower_outputs,
    similarity_sharpness,
    similarity_shift_term,
    objective_upstream_grad,
):
    images, patches, model_width = feedforward_entry_states.shape[1:]
    hidden = stored_hidden_preacts.shape[-1]
    z, y = lax.axis_index("z"), lax.axis_index("y")
    z_size = lax.axis_size("z")
    part = hidden // z_size
    column = images * z_size
    sharpness = similarity_sharpness[0]
    shift = similarity_shift_term[0]
    factor = objective_upstream_grad[0] * sharpness

    up_y = gather_y(expanding_projector[0], y)
    up_whole = lax.all_gather(up_y, "z", axis=0, tiled=True)
    down_y = gather_y(contracting_projector[0], y)

    tokens = feedforward_entry_states[0].reshape(images * patches, model_width).astype(jnp.float32)
    preact = stored_hidden_preacts[0].astype(jnp.float32)
    activated = jax.nn.gelu(preact, approximate=True).astype(jnp.bfloat16).astype(jnp.float32)
    mean_activated = jnp.mean(activated, axis=1)
    mean_high = mean_activated.astype(jnp.bfloat16)
    mean_low = (mean_activated - mean_high.astype(jnp.float32)).astype(jnp.bfloat16)
    mean_tokens = jnp.mean(tokens.reshape(images, patches, model_width), axis=1)

    text_dir, text_inverse = unit_rows(caption_tower_outputs[0].astype(jnp.float32))
    text_unit = text_dir.astype(jnp.bfloat16)

    def by_z(values):
        return values.reshape(images, z_size, part).transpose(1, 0, 2).reshape(z_size, images * part)

    first = exchange_z(
        jnp.concatenate(
            [
                by_z(mean_high),
                by_z(mean_low),
                jnp.broadcast_to(text_unit.reshape(1, -1), (z_size, images * model_width)),
            ],
            axis=1,
        )
    )
    cut = images * part
    column_high = first[:, :cut].reshape(column, part)
    column_low = first[:, cut : 2 * cut].reshape(column, part)
    column_text = first[:, 2 * cut :].reshape(column, model_width)
    text_all = jnp.concatenate(
        [column_text] + [from_ahead(column_text, "y", k) for k in range(1, Y_SHARDS)], axis=0
    )

    partial = jnp.dot(column_high, down_y, preferred_element_type=jnp.float32) + jnp.dot(
        column_low, down_y, preferred_element_type=jnp.float32
    )
    partials = exchange_z(partial.astype(jnp.bfloat16).reshape(z_size, images, model_width))
    pooled = mean_tokens + jnp.sum(partials.astype(jnp.float32), axis=0)
    image_dir, image_inverse = unit_rows(pooled)
    image_unit = image_dir.astype(jnp.bfloat16)

    def index_of(z_index, y_index):
        start = (z_index * Y_SHARDS + y_index % Y_SHARDS) * images
        return start[..., None] + lax.iota(jnp.int32, images)

    text_index = index_of(
        lax.broadcasted_iota(jnp.int32, (Y_SHARDS, z_size), 1),
        y + lax.broadcasted_iota(jnp.int32, (Y_SHARDS, z_size), 0),
    ).reshape(-1)
    weights = pair_weights(
        image_unit, text_all, index_of(z, y).reshape(-1), text_index, sharpness, shift, factor
    )
    image_sum = jnp.dot(weights, text_all, preferred_element_type=jnp.float32)
    pooled_grad = (
        image_sum - image_dir * jnp.sum(image_dir * image_sum, axis=-1, keepdims=True)
    ) * image_inverse
    share = pooled_grad / patches
    token_grad = share.astype(jnp.bfloat16)

    column_grad = exchange_z(jnp.broadcast_to(token_grad[None], (z_size, images, model_width)))
    column_hidden = lax.dot_general(
        column_grad.reshape(column, model_width),
        down_y,
        (((1,), (1,)), ((), ())),
        preferred_element_type=jnp.float32,
    )
    hidden_grad = (
        exchange_z(column_hidden.reshape(z_size, images, part))
        .transpose(1, 0, 2)
        .reshape(images, hidden)
    )

    unit_late, _ = lax.optimization_barrier((image_unit, hidden_grad))
    column_unit = exchange_z(
        jnp.broadcast_to(unit_late[None], (z_size, images, model_width))
    ).reshape(column, model_width)
    row_text = lax.dynamic_index_in_dim(
        text_all.reshape(Y_SHARDS, z_size, images, model_width), z, axis=1, keepdims=False
    ).reshape(Y_SHARDS * images, model_width)
    row_weights = pair_weights(
        column_unit,
        row_text,
        index_of(jnp.arange(z_size, dtype=jnp.int32), y).reshape(-1),
        index_of(z, y + jnp.arange(Y_SHARDS, dtype=jnp.int32)).reshape(-1),
        sharpness,
        shift,
        factor,
    )
    row_sums = lax.dot_general(
        row_weights, column_unit, (((0,), (0,)), ((), ())), preferred_element_type=jnp.float32
    ).reshape(Y_SHARDS, images, model_width)
    text_sum = row_sums[0]
    for k in range(1, Y_SHARDS):
        text_sum = text_sum + from_ahead(row_sums[k], "y", -k)
    text_grad = (
        (text_sum - text_dir * jnp.sum(text_dir * text_sum, axis=-1, keepdims=True)) * text_inverse
    ).astype(jnp.bfloat16)

    preact_grad = (hidden_grad[:, None, :] * gelu_slope(preact)).astype(jnp.bfloat16)
    normed_grad = lax.dot_general(
        preact_grad.reshape(images * patches, hidden),
        up_whole,
        (((1,), (1,)), ((), ())),
        preferred_element_type=jnp.float32,
    )
    inner_grad = norm_backward(tokens, normed_grad, layernorm_multiplier[0]).reshape(
        images, patches, model_width
    )
    span_grad = (share[:, None, :] + inner_grad).astype(jnp.bfloat16)
    prev_grad = from_ahead(span_grad[None], "section", 1)
    return (prev_grad, text_grad[None])


def solution(mesh):
    sections, shards = mesh.devices.shape
    folded = Mesh(
        mesh.devices.reshape(sections, shards // Y_SHARDS, Y_SHARDS), ("section", "z", "y")
    )
    dp = ("z", "y")
    placed = (
        P("section", dp, None, None),
        P("section", dp, None, None),
        P("section", None),
        P("section", dp, None),
        P("section", dp, None),
        P("section", dp, None),
        P(),
        P(),
        P(),
    )
    return jax.shard_map(
        per_device,
        mesh=folded,
        in_specs=placed,
        out_specs=(P("section", dp, None, None), P("section", dp, None)),
        check_vma=False,
    )
```

```python
import jax
import jax.numpy as jnp
from jax import lax
from jax.sharding import Mesh, PartitionSpec as P

EPSILON = 1e-06
TANH_SCALE = 0.7978845608028654
CUBIC_TERM = 0.044715
Y_SHARDS = 4


def from_ahead(array, axis, by):
    peers = lax.axis_size(axis)
    return lax.ppermute(array, axis, [((i + by) % peers, i) for i in range(peers)])


def gelu_slope(preact):
    inner = TANH_SCALE * (preact + CUBIC_TERM * preact * preact * preact)
    tangent = jnp.tanh(inner)
    return 0.5 * (1.0 + tangent) + 0.5 * preact * (1.0 - tangent * tangent) * TANH_SCALE * (
        1.0 + 3.0 * CUBIC_TERM * preact * preact
    )


def unit_rows(values):
    inverse = lax.rsqrt(jnp.sum(values * values, axis=-1, keepdims=True) + EPSILON)
    return (values * inverse, inverse)


def pair_weights(image_unit, text_unit, image_index, text_index, sharpness, shift, factor):
    logits = (
        sharpness
        * lax.dot_general(
            image_unit, text_unit, (((1,), (1,)), ((), ())), preferred_element_type=jnp.float32
        )
        + shift
    )
    signs = jnp.where(image_index[:, None] == text_index[None, :], 1.0, -1.0).astype(jnp.float32)
    return (factor * -signs * jax.nn.sigmoid(-signs * logits)).astype(jnp.bfloat16)


def norm_backward(tokens, normed_grad, layernorm_multiplier):
    centered = tokens - jnp.mean(tokens, axis=-1, keepdims=True)
    inverse = lax.rsqrt(jnp.mean(centered * centered, axis=-1, keepdims=True) + EPSILON)
    normal = centered * inverse
    scaled = normed_grad * layernorm_multiplier
    return inverse * (
        scaled
        - jnp.mean(scaled, axis=-1, keepdims=True)
        - normal * jnp.mean(scaled * normal, axis=-1, keepdims=True)
    )


def exchange_z(blocks):
    return lax.all_to_all(blocks, "z", 0, 0)


def gather_next_section_y(shard, y):
    sections = lax.axis_size("section")

    def pairs(by):
        return [
            (((s + 1) % sections) * Y_SHARDS + (own + by) % Y_SHARDS, s * Y_SHARDS + own)
            for s in range(sections)
            for own in range(Y_SHARDS)
        ]

    ahead = [lax.ppermute(shard, ("section", "y"), pairs(k)) for k in range(Y_SHARDS)]
    placed = [
        lax.select_n(y, *[ahead[(a - own) % Y_SHARDS] for own in range(Y_SHARDS)])
        for a in range(Y_SHARDS)
    ]
    return jnp.concatenate(placed, axis=0)


def per_device(
    feedforward_entry_states,
    stored_hidden_preacts,
    layernorm_multiplier,
    expanding_projector,
    contracting_projector,
    caption_tower_outputs,
    similarity_sharpness,
    similarity_shift_term,
    objective_upstream_grad,
):
    images, patches, model_width = feedforward_entry_states.shape[1:]
    hidden = stored_hidden_preacts.shape[-1]
    z, y = lax.axis_index("z"), lax.axis_index("y")
    z_size = lax.axis_size("z")
    part = hidden // z_size
    column = images * z_size
    sharpness = similarity_sharpness[0]
    shift = similarity_shift_term[0]
    factor = objective_upstream_grad[0] * sharpness

    down_y = lax.all_to_all(
        jnp.broadcast_to(contracting_projector, (Y_SHARDS,) + contracting_projector.shape[1:]),
        "y",
        0,
        0,
    ).reshape(-1, model_width)
    up_y = gather_next_section_y(expanding_projector[0], y)
    up_whole = lax.all_gather(up_y, "z", axis=0, tiled=True)

    tokens = feedforward_entry_states[0].reshape(images * patches, model_width).astype(jnp.float32)
    preact = stored_hidden_preacts[0].astype(jnp.float32)
    activated = jax.nn.gelu(preact, approximate=True).astype(jnp.bfloat16).astype(jnp.float32)
    mean_activated = jnp.mean(activated, axis=1)
    mean_high = mean_activated.astype(jnp.bfloat16)
    mean_low = (mean_activated - mean_high.astype(jnp.float32)).astype(jnp.bfloat16)
    mean_tokens = jnp.mean(tokens.reshape(images, patches, model_width), axis=1)

    text_dir, text_inverse = unit_rows(caption_tower_outputs[0].astype(jnp.float32))
    text_unit = text_dir.astype(jnp.bfloat16)

    def by_z(values):
        return values.reshape(images, z_size, part).transpose(1, 0, 2).reshape(z_size, images * part)

    first = exchange_z(
        jnp.concatenate(
            [
                by_z(mean_high),
                by_z(mean_low),
                jnp.broadcast_to(text_unit.reshape(1, -1), (z_size, images * model_width)),
            ],
            axis=1,
        )
    )
    cut = images * part
    column_high = first[:, :cut].reshape(column, part)
    column_low = first[:, cut : 2 * cut].reshape(column, part)
    column_text = first[:, 2 * cut :].reshape(column, model_width)
    partial = jnp.dot(column_high, down_y, preferred_element_type=jnp.float32) + jnp.dot(
        column_low, down_y, preferred_element_type=jnp.float32
    )
    partial, column_text = lax.optimization_barrier((partial.astype(jnp.bfloat16), column_text))
    text_all = jnp.concatenate(
        [column_text] + [from_ahead(column_text, "y", k) for k in range(1, Y_SHARDS)], axis=0
    )
    partials = exchange_z(partial.reshape(z_size, images, model_width))
    pooled = mean_tokens + jnp.sum(partials.astype(jnp.float32), axis=0)
    image_dir, image_inverse = unit_rows(pooled)
    image_unit = image_dir.astype(jnp.bfloat16)

    text_all, entry_states, preacts = lax.optimization_barrier(
        (text_all, feedforward_entry_states, stored_hidden_preacts)
    )

    def index_of(z_index, y_index):
        start = (z_index * Y_SHARDS + y_index % Y_SHARDS) * images
        return start[..., None] + lax.iota(jnp.int32, images)

    text_index = index_of(
        lax.broadcasted_iota(jnp.int32, (Y_SHARDS, z_size), 1),
        y + lax.broadcasted_iota(jnp.int32, (Y_SHARDS, z_size), 0),
    ).reshape(-1)
    weights = pair_weights(
        image_unit, text_all, index_of(z, y).reshape(-1), text_index, sharpness, shift, factor
    )
    image_sum = jnp.dot(weights, text_all, preferred_element_type=jnp.float32)
    pooled_grad = (
        image_sum - image_dir * jnp.sum(image_dir * image_sum, axis=-1, keepdims=True)
    ) * image_inverse
    share = pooled_grad / patches
    token_grad = share.astype(jnp.bfloat16)

    columns = exchange_z(
        jnp.broadcast_to(
            jnp.concatenate([token_grad, image_unit], axis=0)[None],
            (z_size, 2 * images, model_width),
        )
    )
    column_grad = columns[:, :images].reshape(column, model_width)
    column_unit = columns[:, images:].reshape(column, model_width)
    column_hidden = lax.dot_general(
        column_grad, down_y, (((1,), (1,)), ((), ())), preferred_element_type=jnp.float32
    )
    hidden_grad = (
        exchange_z(column_hidden.reshape(z_size, images, part))
        .transpose(1, 0, 2)
        .reshape(images, hidden)
    )

    row_text = lax.dynamic_index_in_dim(
        text_all.reshape(Y_SHARDS, z_size, images, model_width), z, axis=1, keepdims=False
    ).reshape(Y_SHARDS * images, model_width)
    row_weights = pair_weights(
        column_unit,
        row_text,
        index_of(jnp.arange(z_size, dtype=jnp.int32), y).reshape(-1),
        index_of(z, y + jnp.arange(Y_SHARDS, dtype=jnp.int32)).reshape(-1),
        sharpness,
        shift,
        factor,
    )
    row_sums = lax.dot_general(
        row_weights, column_unit, (((0,), (0,)), ((), ())), preferred_element_type=jnp.float32
    ).reshape(Y_SHARDS, images, model_width)
    text_sum = row_sums[0]
    for k in range(1, Y_SHARDS):
        text_sum = text_sum + from_ahead(row_sums[k], "y", -k)
    text_grad = (
        (text_sum - text_dir * jnp.sum(text_dir * text_sum, axis=-1, keepdims=True)) * text_inverse
    ).astype(jnp.bfloat16)

    next_preact = from_ahead(preacts, "section", 1)[0].astype(jnp.float32)
    next_tokens = from_ahead(entry_states, "section", 1)[0].astype(jnp.float32)
    handed = from_ahead(jnp.concatenate([hidden_grad, share], axis=1), "section", 1)
    next_hidden, next_share = handed[:, :hidden], handed[:, hidden:]
    next_multiplier = from_ahead(layernorm_multiplier, "section", 1)

    preact_grad = (next_hidden[:, None, :] * gelu_slope(next_preact)).astype(jnp.bfloat16)
    normed_grad = lax.dot_general(
        preact_grad.reshape(images * patches, hidden),
        up_whole,
        (((1,), (1,)), ((), ())),
        preferred_element_type=jnp.float32,
    )
    inner_grad = norm_backward(
        next_tokens.reshape(images * patches, model_width), normed_grad, next_multiplier[0]
    ).reshape(images, patches, model_width)
    prev_grad = (next_share[:, None, :] + inner_grad).astype(jnp.bfloat16)[None]
    return (prev_grad, text_grad[None])


def solution(mesh):
    sections, shards = mesh.devices.shape
    folded = Mesh(
        mesh.devices.reshape(sections, shards // Y_SHARDS, Y_SHARDS), ("section", "z", "y")
    )
    dp = ("z", "y")
    placed = (
        P("section", dp, None, None),
        P("section", dp, None, None),
        P("section", None),
        P("section", dp, None),
        P("section", dp, None),
        P("section", dp, None),
        P(),
        P(),
        P(),
    )
    return jax.shard_map(
        per_device,
        mesh=folded,
        in_specs=placed,
        out_specs=(P("section", dp, None, None), P("section", dp, None)),
        check_vma=False,
    )
```

```python
import functools

import jax
import jax.numpy as jnp
from jax import lax
from jax.experimental import pallas as pl
from jax.experimental.pallas import tpu as pltpu
from jax.sharding import Mesh, PartitionSpec as P

EPSILON = 1e-06
TANH_SCALE = 0.7978845608028654
CUBIC_TERM = 0.044715
Y_SHARDS = 4
ROW_TILE = 8
IMAGE_BLOCK = 8
VMEM_BYTES = 50 * 1024 * 1024


def from_ahead(array, axis, by):
    peers = lax.axis_size(axis)
    return lax.ppermute(array, axis, [((i + by) % peers, i) for i in range(peers)])


def gelu_slope(preact):
    inner = TANH_SCALE * (preact + CUBIC_TERM * preact * preact * preact)
    tangent = jnp.tanh(inner)
    return 0.5 * (1.0 + tangent) + 0.5 * preact * (1.0 - tangent * tangent) * TANH_SCALE * (
        1.0 + 3.0 * CUBIC_TERM * preact * preact
    )


def unit_rows(values):
    inverse = lax.rsqrt(jnp.sum(values * values, axis=-1, keepdims=True) + EPSILON)
    return (values * inverse, inverse)


def pair_weights(image_unit, text_unit, image_index, text_index, sharpness, shift, factor):
    logits = (
        sharpness
        * lax.dot_general(
            image_unit, text_unit, (((1,), (1,)), ((), ())), preferred_element_type=jnp.float32
        )
        + shift
    )
    signs = jnp.where(image_index[:, None] == text_index[None, :], 1.0, -1.0).astype(jnp.float32)
    return (factor * -signs * jax.nn.sigmoid(-signs * logits)).astype(jnp.bfloat16)


def norm_backward(tokens, normed_grad, layernorm_multiplier):
    centered = tokens - jnp.mean(tokens, axis=-1, keepdims=True)
    inverse = lax.rsqrt(jnp.mean(centered * centered, axis=-1, keepdims=True) + EPSILON)
    normal = centered * inverse
    scaled = normed_grad * layernorm_multiplier
    return inverse * (
        scaled
        - jnp.mean(scaled, axis=-1, keepdims=True)
        - normal * jnp.mean(scaled * normal, axis=-1, keepdims=True)
    )


def slope_kernel(preact_ref, slope_ref):
    slope_ref[...] = gelu_slope(preact_ref[...].astype(jnp.float32))


def slopes(preact):
    tokens, hidden = preact.shape
    block = tokens // 4
    spec = pl.BlockSpec((block, hidden), lambda i: (i, 0))
    return pl.pallas_call(
        slope_kernel,
        grid=(tokens // block,),
        in_specs=[spec],
        out_specs=spec,
        out_shape=jax.ShapeDtypeStruct((tokens, hidden), jnp.float32),
        compiler_params=pltpu.CompilerParams(vmem_limit_bytes=VMEM_BYTES),
        cost_estimate=pl.CostEstimate(
            flops=20 * tokens * hidden, bytes_accessed=6 * tokens * hidden, transcendentals=0
        ),
    )(preact)


def span_kernel(
    pieces, grad_ref, slope_ref, up_ref, tokens_ref, share_ref, multiplier_ref, span_ref, hidden_ref
):
    @pl.when(pl.program_id(0) == 0)
    def _():
        hidden_ref[...] = jnp.concatenate(
            [grad_ref[y, :, start:end] for y, start, end in pieces], axis=1
        ).reshape(hidden_ref.shape)

    step = pl.program_id(0)
    tokens = tokens_ref[...].astype(jnp.float32)
    rows, width = tokens.shape
    count = IMAGE_BLOCK
    patches = rows // count
    hidden = hidden_ref.shape[2]
    grads = hidden_ref[step]
    slope = slope_ref[...].reshape(count, patches, hidden)
    preact_grad = (grads[:, None, :] * slope).astype(jnp.bfloat16).reshape(rows, hidden)
    normed = lax.dot_general(
        preact_grad, up_ref[...], (((1,), (1,)), ((), ())), preferred_element_type=jnp.float32
    )
    inner = norm_backward(tokens, normed, multiplier_ref[...])
    share = share_ref[step]
    span_ref[...] = (
        (share[:, None, :] + inner.reshape(count, patches, width))
        .astype(jnp.bfloat16)
        .reshape(rows, width)
    )


def span(received, pieces, slope, up_whole, tokens, share, multiplier):
    count, width = tokens.shape
    images = share.shape[0]
    share = share.reshape(images // IMAGE_BLOCK, IMAGE_BLOCK, width)
    hidden = slope.shape[1]
    rows = IMAGE_BLOCK * (count // images)
    whole = lambda array: pl.BlockSpec(array.shape, lambda i: (0,) * array.ndim)
    block = lambda columns: pl.BlockSpec((rows, columns), lambda i: (i, 0))
    return pl.pallas_call(
        functools.partial(span_kernel, pieces),
        grid=(count // rows,),
        in_specs=[
            whole(received),
            block(hidden),
            whole(up_whole),
            block(width),
            whole(share),
            whole(multiplier),
        ],
        out_specs=block(width),
        out_shape=jax.ShapeDtypeStruct((count, width), jnp.bfloat16),
        scratch_shapes=[pltpu.VMEM((images // IMAGE_BLOCK, IMAGE_BLOCK, hidden), jnp.float32)],
        compiler_params=pltpu.CompilerParams(vmem_limit_bytes=VMEM_BYTES),
        cost_estimate=pl.CostEstimate(
            flops=2 * count * hidden * width,
            bytes_accessed=4 * count * hidden + 2 * hidden * width + 4 * count * width,
            transcendentals=0,
        ),
    )(received, slope, up_whole, tokens, share, multiplier)


def exchange_y(blocks):
    return lax.all_to_all(blocks, "y", 0, 0)


def in_order_of_y(ahead, y):
    placed = [
        lax.select_n(y, *[ahead[(a - own) % Y_SHARDS] for own in range(Y_SHARDS)])
        for a in range(Y_SHARDS)
    ]
    return jnp.concatenate(placed, axis=0)


def per_device(
    feedforward_entry_states,
    stored_hidden_preacts,
    layernorm_multiplier,
    expanding_projector,
    contracting_projector,
    caption_tower_outputs,
    similarity_sharpness,
    similarity_shift_term,
    objective_upstream_grad,
):
    images, patches, model_width = feedforward_entry_states.shape[1:]
    hidden = stored_hidden_preacts.shape[-1]
    z, y = lax.axis_index("z"), lax.axis_index("y")
    z_size = lax.axis_size("z")
    shard_rows = contracting_projector.shape[1]
    shard_end = images + shard_rows
    block_rows = -(-shard_end // ROW_TILE) * ROW_TILE
    part = z_size * block_rows
    row = images * Y_SHARDS
    sharpness = similarity_sharpness[0]
    shift = similarity_shift_term[0]
    factor = objective_upstream_grad[0] * sharpness

    block = jnp.concatenate(
        [
            caption_tower_outputs[0],
            contracting_projector[0],
            jnp.zeros((block_rows - shard_end, model_width), jnp.bfloat16),
        ],
        axis=0,
    )
    blocks = lax.all_gather(block, "z", axis=0, tiled=True)

    tokens = feedforward_entry_states[0].reshape(images * patches, model_width).astype(jnp.float32)
    preact = stored_hidden_preacts[0].astype(jnp.float32)
    activated = jax.nn.gelu(preact, approximate=True).astype(jnp.bfloat16).astype(jnp.float32)
    mean_activated = jnp.mean(activated, axis=1)
    mean_tokens = jnp.mean(tokens.reshape(images, patches, model_width), axis=1)

    mean_sent = (
        jnp.pad(
            mean_activated.reshape(images, z_size, Y_SHARDS, shard_rows),
            ((0, 0), (0, 0), (0, 0), (images, block_rows - shard_end)),
        )
        .transpose(2, 0, 1, 3)
        .reshape(Y_SHARDS, images, part)
    )

    mean_sent, up_shard = lax.optimization_barrier((mean_sent, expanding_projector[0]))
    up_y = in_order_of_y(
        [up_shard] + [from_ahead(up_shard, "y", k) for k in range(1, Y_SHARDS)], y
    )
    up_whole = lax.all_gather(up_y, "z", axis=0, tiled=True)

    row_mean = exchange_y(mean_sent).reshape(row, part)
    row_high = row_mean.astype(jnp.bfloat16)
    row_low = (row_mean - row_high.astype(jnp.float32)).astype(jnp.bfloat16)
    partial = jnp.dot(row_high, blocks, preferred_element_type=jnp.float32) + jnp.dot(
        row_low, blocks, preferred_element_type=jnp.float32
    )
    partials = exchange_y(partial.astype(jnp.bfloat16).reshape(Y_SHARDS, images, model_width))
    column_text = blocks.reshape(z_size, block_rows, model_width)[:, :images]
    column_text = unit_rows(
        column_text.reshape(z_size * images, model_width).astype(jnp.float32)
    )[0].astype(jnp.bfloat16)
    text_all = jnp.concatenate(
        [column_text] + [from_ahead(column_text, "y", k) for k in range(1, Y_SHARDS)], axis=0
    )
    pooled = mean_tokens + jnp.sum(partials.astype(jnp.float32), axis=0)
    image_dir, image_inverse = unit_rows(pooled)
    image_unit = image_dir.astype(jnp.bfloat16)

    def index_of(z_index, y_index):
        start = (z_index * Y_SHARDS + y_index) * images
        return start[..., None] + lax.iota(jnp.int32, images)

    def weigh(image_rows, image_index, text_rows, text_index):
        return pair_weights(
            image_rows, text_rows, image_index, text_index, sharpness, shift, factor
        )

    weights = weigh(
        image_unit,
        index_of(z, y).reshape(-1),
        text_all,
        index_of(
            lax.broadcasted_iota(jnp.int32, (Y_SHARDS, z_size), 1),
            (y + lax.broadcasted_iota(jnp.int32, (Y_SHARDS, z_size), 0)) % Y_SHARDS,
        ).reshape(-1),
    )
    image_sum = jnp.dot(weights, text_all, preferred_element_type=jnp.float32)
    pooled_grad = (
        image_sum - image_dir * jnp.sum(image_dir * image_sum, axis=-1, keepdims=True)
    ) * image_inverse
    share = pooled_grad / patches
    token_grad = share.astype(jnp.bfloat16)

    preacts, row_grad = lax.optimization_barrier((stored_hidden_preacts[0], token_grad))
    slope = slopes(preacts.reshape(images * patches, hidden))
    row_sent = jnp.concatenate([row_grad, image_unit], axis=0)
    rows = exchange_y(jnp.broadcast_to(row_sent[None], (Y_SHARDS,) + row_sent.shape))
    row_grad = rows[:, :images].reshape(row, model_width)
    row_unit = rows[:, images:].reshape(row, model_width)
    row_hidden = lax.dot_general(
        row_grad, blocks, (((1,), (1,)), ((), ())), preferred_element_type=jnp.float32
    )
    received = exchange_y(row_hidden.reshape(Y_SHARDS, images, part))
    column_weights = weigh(
        row_unit,
        index_of(z, jnp.arange(Y_SHARDS, dtype=jnp.int32)).reshape(-1),
        column_text,
        index_of(jnp.arange(z_size, dtype=jnp.int32), y).reshape(-1),
    )
    column_sums = lax.dot_general(
        column_weights, row_unit, (((0,), (0,)), ((), ())), preferred_element_type=jnp.float32
    ).reshape(z_size, images, model_width)
    pieces = [
        (own, at * block_rows + images, at * block_rows + shard_end)
        for at in range(z_size)
        for own in range(Y_SHARDS)
    ]
    span_grad = span(
        received,
        pieces,
        slope,
        up_whole,
        feedforward_entry_states.reshape(images * patches, model_width),
        share,
        layernorm_multiplier,
    ).reshape(images, patches, model_width)
    column_sums, span_grad = lax.optimization_barrier((column_sums, span_grad))
    text_sums = lax.all_to_all(column_sums, "z", 0, 0)
    prev_grad = from_ahead(span_grad[None], "section", 1)

    text_sum = jnp.sum(text_sums, axis=0)
    text_dir, text_inverse = unit_rows(caption_tower_outputs[0].astype(jnp.float32))
    text_grad = (
        (text_sum - text_dir * jnp.sum(text_dir * text_sum, axis=-1, keepdims=True)) * text_inverse
    ).astype(jnp.bfloat16)
    return (prev_grad, text_grad[None])


def solution(mesh):
    sections, shards = mesh.devices.shape
    folded = Mesh(
        mesh.devices.reshape(sections, shards // Y_SHARDS, Y_SHARDS), ("section", "z", "y")
    )
    dp = ("z", "y")
    placed = (
        P("section", dp, None, None),
        P("section", dp, None, None),
        P("section", None),
        P("section", dp, None),
        P("section", dp, None),
        P("section", dp, None),
        P(),
        P(),
        P(),
    )
    return jax.shard_map(
        per_device,
        mesh=folded,
        in_specs=placed,
        out_specs=(P("section", dp, None, None), P("section", dp, None)),
        check_vma=False,
    )
```

```python
import functools

import jax
import jax.numpy as jnp
from jax import lax
from jax.experimental import pallas as pl
from jax.experimental.pallas import tpu as pltpu
from jax.sharding import Mesh, PartitionSpec as P

EPSILON = 1e-06
TANH_SCALE = 0.7978845608028654
CUBIC_TERM = 0.044715
Y_SHARDS = 4
ROW_TILE = 8
IMAGE_BLOCK = 8
VMEM_BYTES = 50 * 1024 * 1024


def from_ahead(array, axis, by):
    peers = lax.axis_size(axis)
    return lax.ppermute(array, axis, [((i + by) % peers, i) for i in range(peers)])


def gelu_slope(preact):
    inner = TANH_SCALE * (preact + CUBIC_TERM * preact * preact * preact)
    tangent = jnp.tanh(inner)
    return 0.5 * (1.0 + tangent) + 0.5 * preact * (1.0 - tangent * tangent) * TANH_SCALE * (
        1.0 + 3.0 * CUBIC_TERM * preact * preact
    )


def unit_rows(values):
    inverse = lax.rsqrt(jnp.sum(values * values, axis=-1, keepdims=True) + EPSILON)
    return (values * inverse, inverse)


def pair_weights(image_unit, text_unit, image_index, text_index, sharpness, shift, factor):
    logits = (
        sharpness
        * lax.dot_general(
            image_unit, text_unit, (((1,), (1,)), ((), ())), preferred_element_type=jnp.float32
        )
        + shift
    )
    signs = jnp.where(image_index[:, None] == text_index[None, :], 1.0, -1.0).astype(jnp.float32)
    return (factor * -signs * jax.nn.sigmoid(-signs * logits)).astype(jnp.bfloat16)


def norm_backward(tokens, normed_grad, layernorm_multiplier):
    centered = tokens - jnp.mean(tokens, axis=-1, keepdims=True)
    inverse = lax.rsqrt(jnp.mean(centered * centered, axis=-1, keepdims=True) + EPSILON)
    normal = centered * inverse
    scaled = normed_grad * layernorm_multiplier
    return inverse * (
        scaled
        - jnp.mean(scaled, axis=-1, keepdims=True)
        - normal * jnp.mean(scaled * normal, axis=-1, keepdims=True)
    )


def partial_kernel(means_ref, blocks_ref, sums_ref):
    means = means_ref[...]
    high = means.astype(jnp.bfloat16)
    low = (means - high.astype(jnp.float32)).astype(jnp.bfloat16)
    blocks = blocks_ref[...]
    sums = jnp.dot(high, blocks, preferred_element_type=jnp.float32)
    sums = sums + jnp.dot(low, blocks, preferred_element_type=jnp.float32)
    sums_ref[...] = sums.astype(jnp.bfloat16)


def back_kernel(grads_ref, blocks_ref, sums_ref, sent_ref):
    width = sums_ref.shape[1]
    hidden = lax.dot_general(
        grads_ref[...], blocks_ref[...], (((1,), (1,)), ((), ())), preferred_element_type=jnp.float32
    )
    sent_ref[:, :width] = sums_ref[...].astype(jnp.bfloat16)
    sent_ref[:, width:] = hidden.astype(jnp.bfloat16)


def small_call(kernel, rows, columns, operands, flops):
    return pl.pallas_call(
        kernel,
        out_shape=jax.ShapeDtypeStruct((rows, columns), jnp.bfloat16),
        in_specs=[pl.BlockSpec(memory_space=pltpu.VMEM)] * len(operands),
        out_specs=pl.BlockSpec(memory_space=pltpu.VMEM),
        compiler_params=pltpu.CompilerParams(vmem_limit_bytes=VMEM_BYTES),
        cost_estimate=pl.CostEstimate(flops=flops, bytes_accessed=2000000, transcendentals=0),
    )(*operands)


def slope_kernel(preact_ref, slope_ref):
    slope_ref[...] = gelu_slope(preact_ref[...].astype(jnp.float32))


def slopes(preact):
    tokens, hidden = preact.shape
    block = tokens // 4
    spec = pl.BlockSpec((block, hidden), lambda i: (i, 0))
    return pl.pallas_call(
        slope_kernel,
        grid=(tokens // block,),
        in_specs=[spec],
        out_specs=spec,
        out_shape=jax.ShapeDtypeStruct((tokens, hidden), jnp.float32),
        compiler_params=pltpu.CompilerParams(vmem_limit_bytes=VMEM_BYTES),
        cost_estimate=pl.CostEstimate(
            flops=20 * tokens * hidden, bytes_accessed=6 * tokens * hidden, transcendentals=0
        ),
    )(preact)


def span_kernel(
    pieces, grad_ref, slope_ref, up_ref, tokens_ref, share_ref, multiplier_ref, span_ref, hidden_ref
):
    @pl.when(pl.program_id(0) == 0)
    def _():
        hidden_ref[...] = jnp.concatenate(
            [grad_ref[y, :, start:end].astype(jnp.float32) for y, start, end in pieces], axis=1
        ).reshape(hidden_ref.shape)

    step = pl.program_id(0)
    tokens = tokens_ref[...].astype(jnp.float32)
    rows, width = tokens.shape
    count = IMAGE_BLOCK
    patches = rows // count
    hidden = hidden_ref.shape[2]
    grads = hidden_ref[step]
    slope = slope_ref[...].reshape(count, patches, hidden)
    preact_grad = (grads[:, None, :] * slope).astype(jnp.bfloat16).reshape(rows, hidden)
    normed = lax.dot_general(
        preact_grad, up_ref[...], (((1,), (1,)), ((), ())), preferred_element_type=jnp.float32
    )
    inner = norm_backward(tokens, normed, multiplier_ref[...])
    share = share_ref[step]
    span_ref[...] = (
        (share[:, None, :] + inner.reshape(count, patches, width))
        .astype(jnp.bfloat16)
        .reshape(rows, width)
    )


def span(received, pieces, slope, up_whole, tokens, share, multiplier):
    count, width = tokens.shape
    images = share.shape[0]
    share = share.reshape(images // IMAGE_BLOCK, IMAGE_BLOCK, width)
    hidden = slope.shape[1]
    rows = IMAGE_BLOCK * (count // images)
    whole = lambda array: pl.BlockSpec(array.shape, lambda i: (0,) * array.ndim)
    block = lambda columns: pl.BlockSpec((rows, columns), lambda i: (i, 0))
    return pl.pallas_call(
        functools.partial(span_kernel, pieces),
        grid=(count // rows,),
        in_specs=[
            whole(received),
            block(hidden),
            whole(up_whole),
            block(width),
            whole(share),
            whole(multiplier),
        ],
        out_specs=block(width),
        out_shape=jax.ShapeDtypeStruct((count, width), jnp.bfloat16),
        scratch_shapes=[pltpu.VMEM((images // IMAGE_BLOCK, IMAGE_BLOCK, hidden), jnp.float32)],
        compiler_params=pltpu.CompilerParams(vmem_limit_bytes=VMEM_BYTES),
        cost_estimate=pl.CostEstimate(
            flops=2 * count * hidden * width,
            bytes_accessed=4 * count * hidden + 2 * hidden * width + 4 * count * width,
            transcendentals=0,
        ),
    )(received, slope, up_whole, tokens, share, multiplier)


def exchange_y(blocks):
    return lax.all_to_all(blocks, "y", 0, 0)


def in_order_of_y(ahead, y):
    placed = [
        lax.select_n(y, *[ahead[(a - own) % Y_SHARDS] for own in range(Y_SHARDS)])
        for a in range(Y_SHARDS)
    ]
    return jnp.concatenate(placed, axis=0)


def per_device(
    feedforward_entry_states,
    stored_hidden_preacts,
    layernorm_multiplier,
    expanding_projector,
    contracting_projector,
    caption_tower_outputs,
    similarity_sharpness,
    similarity_shift_term,
    objective_upstream_grad,
):
    images, patches, model_width = feedforward_entry_states.shape[1:]
    hidden = stored_hidden_preacts.shape[-1]
    z, y = lax.axis_index("z"), lax.axis_index("y")
    z_size = lax.axis_size("z")
    shard_rows = contracting_projector.shape[1]
    shard_end = images + shard_rows
    block_rows = -(-shard_end // ROW_TILE) * ROW_TILE
    part = z_size * block_rows
    row = images * Y_SHARDS
    sharpness = similarity_sharpness[0]
    shift = similarity_shift_term[0]
    factor = objective_upstream_grad[0] * sharpness

    block = jnp.concatenate(
        [
            caption_tower_outputs[0],
            contracting_projector[0],
            jnp.zeros((block_rows - shard_end, model_width), jnp.bfloat16),
        ],
        axis=0,
    )
    blocks = lax.all_gather(block, "z", axis=0, tiled=True)

    tokens = feedforward_entry_states[0].reshape(images * patches, model_width).astype(jnp.float32)
    preact = stored_hidden_preacts[0].astype(jnp.float32)
    activated = jax.nn.gelu(preact, approximate=True).astype(jnp.bfloat16).astype(jnp.float32)
    mean_activated = jnp.mean(activated, axis=1)
    mean_tokens = jnp.mean(tokens.reshape(images, patches, model_width), axis=1)

    mean_sent = (
        jnp.pad(
            mean_activated.reshape(images, z_size, Y_SHARDS, shard_rows),
            ((0, 0), (0, 0), (0, 0), (images, block_rows - shard_end)),
        )
        .transpose(2, 0, 1, 3)
        .reshape(Y_SHARDS, images, part)
    )

    mean_sent, up_shard = lax.optimization_barrier((mean_sent, expanding_projector[0]))
    up_y = in_order_of_y(
        [up_shard] + [from_ahead(up_shard, "y", k) for k in range(1, Y_SHARDS)], y
    )
    up_whole = lax.all_gather(up_y, "z", axis=0, tiled=True)

    row_mean = exchange_y(mean_sent).reshape(row, part)
    partial = small_call(
        partial_kernel, row, model_width, (row_mean, blocks), 4 * row * part * model_width
    )
    partials = exchange_y(partial.reshape(Y_SHARDS, images, model_width))
    column_text = blocks.reshape(z_size, block_rows, model_width)[:, :images]
    column_text = unit_rows(
        column_text.reshape(z_size * images, model_width).astype(jnp.float32)
    )[0].astype(jnp.bfloat16)
    text_all = jnp.concatenate(
        [column_text] + [from_ahead(column_text, "y", k) for k in range(1, Y_SHARDS)], axis=0
    )
    pooled = mean_tokens + jnp.sum(partials.astype(jnp.float32), axis=0)
    image_dir, image_inverse = unit_rows(pooled)
    image_unit = image_dir.astype(jnp.bfloat16)
    column_unit = lax.all_to_all(
        jnp.broadcast_to(image_unit[None], (z_size, images, model_width)), "z", 0, 0
    ).reshape(z_size * images, model_width)

    def index_of(z_index, y_index):
        start = (z_index * Y_SHARDS + y_index) * images
        return start[..., None] + lax.iota(jnp.int32, images)

    def weigh(image_rows, image_index, text_rows, text_index):
        return pair_weights(
            image_rows, text_rows, image_index, text_index, sharpness, shift, factor
        )

    weights = weigh(
        image_unit,
        index_of(z, y).reshape(-1),
        text_all,
        index_of(
            lax.broadcasted_iota(jnp.int32, (Y_SHARDS, z_size), 1),
            (y + lax.broadcasted_iota(jnp.int32, (Y_SHARDS, z_size), 0)) % Y_SHARDS,
        ).reshape(-1),
    )
    image_sum = jnp.dot(weights, text_all, preferred_element_type=jnp.float32)
    pooled_grad = (
        image_sum - image_dir * jnp.sum(image_dir * image_sum, axis=-1, keepdims=True)
    ) * image_inverse
    share = pooled_grad / patches
    token_grad = share.astype(jnp.bfloat16)

    column_unit, token_grad = lax.optimization_barrier((column_unit, token_grad))
    row_grad = exchange_y(
        jnp.broadcast_to(token_grad[None], (Y_SHARDS,) + token_grad.shape)
    ).reshape(row, model_width)
    preacts, column_unit = lax.optimization_barrier((stored_hidden_preacts[0], column_unit))
    slope = slopes(preacts.reshape(images * patches, hidden))
    row_text = lax.dynamic_index_in_dim(
        text_all.reshape(Y_SHARDS, z_size, images, model_width), z, axis=1, keepdims=False
    )
    row_text = in_order_of_y([row_text[k] for k in range(Y_SHARDS)], y)
    row_weights = weigh(
        column_unit,
        index_of(jnp.arange(z_size, dtype=jnp.int32), y).reshape(-1),
        row_text,
        index_of(z, jnp.arange(Y_SHARDS, dtype=jnp.int32)).reshape(-1),
    )
    row_sums = lax.dot_general(
        row_weights, column_unit, (((0,), (0,)), ((), ())), preferred_element_type=jnp.float32
    )
    sent_back = small_call(
        back_kernel, row, model_width + part, (row_grad, blocks, row_sums), 2 * row * part * model_width
    )
    received = exchange_y(sent_back.reshape(Y_SHARDS, images, model_width + part))
    text_sum = jnp.sum(received[:, :, :model_width].astype(jnp.float32), axis=0)
    pieces = [
        (
            own,
            model_width + at * block_rows + images,
            model_width + at * block_rows + shard_end,
        )
        for at in range(z_size)
        for own in range(Y_SHARDS)
    ]
    span_grad = span(
        received,
        pieces,
        slope,
        up_whole,
        feedforward_entry_states.reshape(images * patches, model_width),
        share,
        layernorm_multiplier,
    ).reshape(images, patches, model_width)
    prev_grad = from_ahead(span_grad[None], "section", 1)

    text_dir, text_inverse = unit_rows(caption_tower_outputs[0].astype(jnp.float32))
    text_grad = (
        (text_sum - text_dir * jnp.sum(text_dir * text_sum, axis=-1, keepdims=True)) * text_inverse
    ).astype(jnp.bfloat16)
    return (prev_grad, text_grad[None])


def solution(mesh):
    sections, shards = mesh.devices.shape
    folded = Mesh(
        mesh.devices.reshape(sections, shards // Y_SHARDS, Y_SHARDS), ("section", "z", "y")
    )
    dp = ("z", "y")
    placed = (
        P("section", dp, None, None),
        P("section", dp, None, None),
        P("section", None),
        P("section", dp, None),
        P("section", dp, None),
        P("section", dp, None),
        P(),
        P(),
        P(),
    )
    return jax.shard_map(
        per_device,
        mesh=folded,
        in_specs=placed,
        out_specs=(P("section", dp, None, None), P("section", dp, None)),
        check_vma=False,
    )
```

```python
import functools

import jax
import jax.numpy as jnp
from jax import lax
from jax.experimental import pallas as pl
from jax.experimental.pallas import tpu as pltpu
from jax.sharding import Mesh, PartitionSpec as P

EPSILON = 1e-06
TANH_SCALE = 0.7978845608028654
CUBIC_TERM = 0.044715
Y_SHARDS = 4
ROW_TILE = 8
IMAGE_BLOCK = 8
VMEM_BYTES = 50 * 1024 * 1024


def from_ahead(array, axis, by):
    peers = lax.axis_size(axis)
    return lax.ppermute(array, axis, [((i + by) % peers, i) for i in range(peers)])


def gelu_slope(preact):
    inner = TANH_SCALE * (preact + CUBIC_TERM * preact * preact * preact)
    tangent = jnp.tanh(inner)
    return 0.5 * (1.0 + tangent) + 0.5 * preact * (1.0 - tangent * tangent) * TANH_SCALE * (
        1.0 + 3.0 * CUBIC_TERM * preact * preact
    )


def unit_rows(values):
    inverse = lax.rsqrt(jnp.sum(values * values, axis=-1, keepdims=True) + EPSILON)
    return (values * inverse, inverse)


def pair_weights(image_unit, text_unit, image_index, text_index, sharpness, shift, factor):
    logits = (
        sharpness
        * lax.dot_general(
            image_unit, text_unit, (((1,), (1,)), ((), ())), preferred_element_type=jnp.float32
        )
        + shift
    )
    signs = jnp.where(image_index[:, None] == text_index[None, :], 1.0, -1.0).astype(jnp.float32)
    return (factor * -signs * jax.nn.sigmoid(-signs * logits)).astype(jnp.bfloat16)


def norm_backward(tokens, normed_grad, layernorm_multiplier):
    centered = tokens - jnp.mean(tokens, axis=-1, keepdims=True)
    inverse = lax.rsqrt(jnp.mean(centered * centered, axis=-1, keepdims=True) + EPSILON)
    normal = centered * inverse
    scaled = normed_grad * layernorm_multiplier
    return inverse * (
        scaled
        - jnp.mean(scaled, axis=-1, keepdims=True)
        - normal * jnp.mean(scaled * normal, axis=-1, keepdims=True)
    )


def partial_kernel(means_ref, blocks_ref, own_ref, sums_ref):
    means = means_ref[...]
    high = means.astype(jnp.bfloat16)
    low = (means - high.astype(jnp.float32)).astype(jnp.bfloat16)
    blocks = blocks_ref[...]
    sums = jnp.dot(high, blocks, preferred_element_type=jnp.float32)
    sums = sums + jnp.dot(low, blocks, preferred_element_type=jnp.float32)
    sums_ref[...] = (sums + own_ref[...]).astype(jnp.bfloat16)


def back_kernel(grads_ref, blocks_ref, sent_ref):
    hidden = lax.dot_general(
        grads_ref[...], blocks_ref[...], (((1,), (1,)), ((), ())), preferred_element_type=jnp.float32
    )
    sent_ref[...] = hidden.astype(jnp.bfloat16)


def small_call(kernel, rows, columns, operands, flops):
    return pl.pallas_call(
        kernel,
        out_shape=jax.ShapeDtypeStruct((rows, columns), jnp.bfloat16),
        in_specs=[pl.BlockSpec(memory_space=pltpu.VMEM)] * len(operands),
        out_specs=pl.BlockSpec(memory_space=pltpu.VMEM),
        compiler_params=pltpu.CompilerParams(vmem_limit_bytes=VMEM_BYTES),
        cost_estimate=pl.CostEstimate(flops=flops, bytes_accessed=2000000, transcendentals=0),
    )(*operands)


def slope_kernel(preact_ref, slope_ref):
    slope_ref[...] = gelu_slope(preact_ref[...].astype(jnp.float32))


def slopes(preact):
    tokens, hidden = preact.shape
    block = tokens // 4
    spec = pl.BlockSpec((block, hidden), lambda i: (i, 0))
    return pl.pallas_call(
        slope_kernel,
        grid=(tokens // block,),
        in_specs=[spec],
        out_specs=spec,
        out_shape=jax.ShapeDtypeStruct((tokens, hidden), jnp.float32),
        compiler_params=pltpu.CompilerParams(vmem_limit_bytes=VMEM_BYTES),
        cost_estimate=pl.CostEstimate(
            flops=20 * tokens * hidden, bytes_accessed=6 * tokens * hidden, transcendentals=0
        ),
    )(preact)


def span_kernel(
    pieces, grad_ref, slope_ref, up_ref, tokens_ref, share_ref, multiplier_ref, span_ref, hidden_ref
):
    @pl.when(pl.program_id(0) == 0)
    def _():
        hidden_ref[...] = jnp.concatenate(
            [grad_ref[y, :, start:end].astype(jnp.float32) for y, start, end in pieces], axis=1
        ).reshape(hidden_ref.shape)

    step = pl.program_id(0)
    tokens = tokens_ref[...].astype(jnp.float32)
    rows, width = tokens.shape
    count = IMAGE_BLOCK
    patches = rows // count
    hidden = hidden_ref.shape[2]
    grads = hidden_ref[step]
    slope = slope_ref[...].reshape(count, patches, hidden)
    preact_grad = (grads[:, None, :] * slope).astype(jnp.bfloat16).reshape(rows, hidden)
    normed = lax.dot_general(
        preact_grad, up_ref[...], (((1,), (1,)), ((), ())), preferred_element_type=jnp.float32
    )
    inner = norm_backward(tokens, normed, multiplier_ref[...])
    share = share_ref[step]
    span_ref[...] = (
        (share[:, None, :] + inner.reshape(count, patches, width))
        .astype(jnp.bfloat16)
        .reshape(rows, width)
    )


def span(received, pieces, slope, up_whole, tokens, share, multiplier):
    count, width = tokens.shape
    images = share.shape[0]
    share = share.reshape(images // IMAGE_BLOCK, IMAGE_BLOCK, width)
    hidden = slope.shape[1]
    rows = IMAGE_BLOCK * (count // images)
    whole = lambda array: pl.BlockSpec(array.shape, lambda i: (0,) * array.ndim)
    block = lambda columns: pl.BlockSpec((rows, columns), lambda i: (i, 0))
    return pl.pallas_call(
        functools.partial(span_kernel, pieces),
        grid=(count // rows,),
        in_specs=[
            whole(received),
            block(hidden),
            whole(up_whole),
            block(width),
            whole(share),
            whole(multiplier),
        ],
        out_specs=block(width),
        out_shape=jax.ShapeDtypeStruct((count, width), jnp.bfloat16),
        scratch_shapes=[pltpu.VMEM((images // IMAGE_BLOCK, IMAGE_BLOCK, hidden), jnp.float32)],
        compiler_params=pltpu.CompilerParams(vmem_limit_bytes=VMEM_BYTES),
        cost_estimate=pl.CostEstimate(
            flops=2 * count * hidden * width,
            bytes_accessed=4 * count * hidden + 2 * hidden * width + 4 * count * width,
            transcendentals=0,
        ),
    )(received, slope, up_whole, tokens, share, multiplier)


def exchange_y(blocks):
    return lax.all_to_all(blocks, "y", 0, 0)


def in_order_of_y(ahead, y):
    placed = [
        lax.select_n(y, *[ahead[(a - own) % Y_SHARDS] for own in range(Y_SHARDS)])
        for a in range(Y_SHARDS)
    ]
    return jnp.concatenate(placed, axis=0)


def per_device(
    feedforward_entry_states,
    stored_hidden_preacts,
    layernorm_multiplier,
    expanding_projector,
    contracting_projector,
    caption_tower_outputs,
    similarity_sharpness,
    similarity_shift_term,
    objective_upstream_grad,
):
    images, patches, model_width = feedforward_entry_states.shape[1:]
    hidden = stored_hidden_preacts.shape[-1]
    z, y = lax.axis_index("z"), lax.axis_index("y")
    z_size = lax.axis_size("z")
    shard_rows = contracting_projector.shape[1]
    shard_end = images + shard_rows
    block_rows = -(-shard_end // ROW_TILE) * ROW_TILE
    part = z_size * block_rows
    row = images * Y_SHARDS
    sharpness = similarity_sharpness[0]
    shift = similarity_shift_term[0]
    factor = objective_upstream_grad[0] * sharpness

    block = jnp.concatenate(
        [
            caption_tower_outputs[0],
            contracting_projector[0],
            jnp.zeros((block_rows - shard_end, model_width), jnp.bfloat16),
        ],
        axis=0,
    )
    blocks = lax.all_gather(block, "z", axis=0, tiled=True)

    tokens = feedforward_entry_states[0].reshape(images * patches, model_width).astype(jnp.float32)
    preact = stored_hidden_preacts[0].astype(jnp.float32)
    activated = jax.nn.gelu(preact, approximate=True).astype(jnp.bfloat16).astype(jnp.float32)
    mean_activated = jnp.mean(activated, axis=1)
    mean_tokens = jnp.mean(tokens.reshape(images, patches, model_width), axis=1)

    mean_sent = (
        jnp.pad(
            mean_activated.reshape(images, z_size, Y_SHARDS, shard_rows),
            ((0, 0), (0, 0), (0, 0), (images, block_rows - shard_end)),
        )
        .transpose(2, 0, 1, 3)
        .reshape(Y_SHARDS, images, part)
    )

    mean_sent, up_shard = lax.optimization_barrier((mean_sent, expanding_projector[0]))
    up_y = in_order_of_y(
        [up_shard] + [from_ahead(up_shard, "y", k) for k in range(1, Y_SHARDS)], y
    )
    up_whole = lax.all_gather(up_y, "z", axis=0, tiled=True)

    row_mean = exchange_y(mean_sent).reshape(row, part)
    own_means = jnp.where(
        jnp.arange(Y_SHARDS, dtype=jnp.int32)[:, None, None] == y, mean_tokens[None], 0.0
    ).reshape(row, model_width)
    partial = small_call(
        partial_kernel,
        row,
        model_width,
        (row_mean, blocks, own_means),
        4 * row * part * model_width,
    )
    partials = exchange_y(jnp.broadcast_to(partial[None], (Y_SHARDS, row, model_width)))
    column_text = blocks.reshape(z_size, block_rows, model_width)[:, :images]
    column_text = unit_rows(
        column_text.reshape(z_size * images, model_width).astype(jnp.float32)
    )[0].astype(jnp.bfloat16)
    text_all = jnp.concatenate(
        [column_text] + [from_ahead(column_text, "y", k) for k in range(1, Y_SHARDS)], axis=0
    )
    pooled = jnp.sum(partials.astype(jnp.float32), axis=0)
    image_dir, image_inverse = unit_rows(pooled)
    image_unit = image_dir.astype(jnp.bfloat16)

    def index_of(z_index, y_index):
        start = (z_index * Y_SHARDS + y_index) * images
        return start[..., None] + lax.iota(jnp.int32, images)

    def weigh(image_rows, image_index, text_rows, text_index):
        return pair_weights(
            image_rows, text_rows, image_index, text_index, sharpness, shift, factor
        )

    weights = weigh(
        image_unit,
        index_of(z, jnp.arange(Y_SHARDS, dtype=jnp.int32)).reshape(-1),
        text_all,
        index_of(
            lax.broadcasted_iota(jnp.int32, (Y_SHARDS, z_size), 1),
            (y + lax.broadcasted_iota(jnp.int32, (Y_SHARDS, z_size), 0)) % Y_SHARDS,
        ).reshape(-1),
    )
    image_sum = jnp.dot(weights, text_all, preferred_element_type=jnp.float32)
    pooled_grad = (
        image_sum - image_dir * jnp.sum(image_dir * image_sum, axis=-1, keepdims=True)
    ) * image_inverse
    row_share = pooled_grad / patches
    row_grad = row_share.astype(jnp.bfloat16)
    share = lax.dynamic_slice_in_dim(row_share, y * images, images, axis=0)
    preacts, row_grad = lax.optimization_barrier((stored_hidden_preacts[0], row_grad))
    slope = slopes(preacts.reshape(images * patches, hidden))
    sent_back = small_call(
        back_kernel, row, part, (row_grad, blocks), 2 * row * part * model_width
    )
    received = exchange_y(sent_back.reshape(Y_SHARDS, images, part))
    column_sums = lax.dot_general(
        weights[:, : z_size * images],
        image_unit,
        (((0,), (0,)), ((), ())),
        preferred_element_type=jnp.float32,
    )
    column_sums, received = lax.optimization_barrier(
        (column_sums.astype(jnp.bfloat16), received)
    )
    text_sums = lax.all_to_all(
        column_sums.reshape(z_size, images, model_width), "z", 0, 0
    )
    text_sum = jnp.sum(text_sums.astype(jnp.float32), axis=0)
    pieces = [
        (
            own,
            at * block_rows + images,
            at * block_rows + shard_end,
        )
        for at in range(z_size)
        for own in range(Y_SHARDS)
    ]
    span_grad = span(
        received,
        pieces,
        slope,
        up_whole,
        feedforward_entry_states.reshape(images * patches, model_width),
        share,
        layernorm_multiplier,
    ).reshape(images, patches, model_width)
    prev_grad = from_ahead(span_grad[None], "section", 1)

    text_dir, text_inverse = unit_rows(caption_tower_outputs[0].astype(jnp.float32))
    text_grad = (
        (text_sum - text_dir * jnp.sum(text_dir * text_sum, axis=-1, keepdims=True)) * text_inverse
    ).astype(jnp.bfloat16)
    return (prev_grad, text_grad[None])


def solution(mesh):
    sections, shards = mesh.devices.shape
    folded = Mesh(
        mesh.devices.reshape(sections, shards // Y_SHARDS, Y_SHARDS), ("section", "z", "y")
    )
    dp = ("z", "y")
    placed = (
        P("section", dp, None, None),
        P("section", dp, None, None),
        P("section", None),
        P("section", dp, None),
        P("section", dp, None),
        P("section", dp, None),
        P(),
        P(),
        P(),
    )
    return jax.shard_map(
        per_device,
        mesh=folded,
        in_specs=placed,
        out_specs=(P("section", dp, None, None), P("section", dp, None)),
        check_vma=False,
    )
```

```python
import functools

import jax
import jax.numpy as jnp
from jax import lax
from jax.experimental import pallas as pl
from jax.experimental.pallas import tpu as pltpu
from jax.sharding import Mesh, PartitionSpec as P

EPSILON = 1e-06
TANH_SCALE = 0.7978845608028654
CUBIC_TERM = 0.044715
Y_SHARDS = 4
ROW_TILE = 8
IMAGE_BLOCK = 8
VMEM_BYTES = 50 * 1024 * 1024


def from_ahead(array, axis, by):
    peers = lax.axis_size(axis)
    return lax.ppermute(array, axis, [((i + by) % peers, i) for i in range(peers)])


def gelu_slope(preact):
    inner = TANH_SCALE * (preact + CUBIC_TERM * preact * preact * preact)
    tangent = jnp.tanh(inner)
    return 0.5 * (1.0 + tangent) + 0.5 * preact * (1.0 - tangent * tangent) * TANH_SCALE * (
        1.0 + 3.0 * CUBIC_TERM * preact * preact
    )


def unit_rows(values):
    inverse = lax.rsqrt(jnp.sum(values * values, axis=-1, keepdims=True) + EPSILON)
    return (values * inverse, inverse)


def pair_weights(image_unit, text_unit, image_index, text_index, sharpness, shift, factor):
    logits = (
        sharpness
        * lax.dot_general(
            image_unit, text_unit, (((1,), (1,)), ((), ())), preferred_element_type=jnp.float32
        )
        + shift
    )
    signs = jnp.where(image_index[:, None] == text_index[None, :], 1.0, -1.0).astype(jnp.float32)
    return (factor * -signs * jax.nn.sigmoid(-signs * logits)).astype(jnp.bfloat16)


def norm_backward(tokens, normed_grad, layernorm_multiplier):
    centered = tokens - jnp.mean(tokens, axis=-1, keepdims=True)
    inverse = lax.rsqrt(jnp.mean(centered * centered, axis=-1, keepdims=True) + EPSILON)
    normal = centered * inverse
    scaled = normed_grad * layernorm_multiplier
    return inverse * (
        scaled
        - jnp.mean(scaled, axis=-1, keepdims=True)
        - normal * jnp.mean(scaled * normal, axis=-1, keepdims=True)
    )


def partial_kernel(images, means_ref, blocks_ref, own_ref, sent_ref):
    means = means_ref[...]
    high = means.astype(jnp.bfloat16)
    low = (means - high.astype(jnp.float32)).astype(jnp.bfloat16)
    blocks = blocks_ref[...]
    sums = jnp.dot(high, blocks, preferred_element_type=jnp.float32)
    sums = sums + jnp.dot(low, blocks, preferred_element_type=jnp.float32)
    sums = (sums + own_ref[...]).astype(jnp.bfloat16)
    rows, width = sums.shape
    blocks_z = sent_ref.shape[1] // images - rows // images
    block_rows = blocks.shape[0] // blocks_z
    for at in range(blocks_z):
        text = blocks[at * block_rows : at * block_rows + images].astype(jnp.float32)
        inverse = lax.rsqrt(jnp.sum(text * text, axis=-1, keepdims=True) + EPSILON)
        unit = (text * inverse).astype(jnp.bfloat16)
        for peer in range(sent_ref.shape[0]):
            sent_ref[peer, rows + at * images : rows + (at + 1) * images] = unit
    for peer in range(sent_ref.shape[0]):
        sent_ref[peer, :rows] = sums


def back_kernel(grads_ref, blocks_ref, sent_ref):
    hidden = lax.dot_general(
        grads_ref[...], blocks_ref[...], (((1,), (1,)), ((), ())), preferred_element_type=jnp.float32
    )
    sent_ref[...] = hidden.astype(jnp.bfloat16)


def small_call(kernel, shape, operands, flops):
    return pl.pallas_call(
        kernel,
        out_shape=jax.ShapeDtypeStruct(shape, jnp.bfloat16),
        in_specs=[pl.BlockSpec(memory_space=pltpu.VMEM)] * len(operands),
        out_specs=pl.BlockSpec(memory_space=pltpu.VMEM),
        compiler_params=pltpu.CompilerParams(vmem_limit_bytes=VMEM_BYTES),
        cost_estimate=pl.CostEstimate(flops=flops, bytes_accessed=2000000, transcendentals=0),
    )(*operands)


def slope_kernel(preact_ref, slope_ref):
    slope_ref[...] = gelu_slope(preact_ref[...].astype(jnp.float32))


def slopes(preact):
    tokens, hidden = preact.shape
    block = tokens // 4
    spec = pl.BlockSpec((block, hidden), lambda i: (i, 0))
    return pl.pallas_call(
        slope_kernel,
        grid=(tokens // block,),
        in_specs=[spec],
        out_specs=spec,
        out_shape=jax.ShapeDtypeStruct((tokens, hidden), jnp.float32),
        compiler_params=pltpu.CompilerParams(vmem_limit_bytes=VMEM_BYTES),
        cost_estimate=pl.CostEstimate(
            flops=20 * tokens * hidden, bytes_accessed=6 * tokens * hidden, transcendentals=0
        ),
    )(preact)


def span_kernel(
    pieces, grad_ref, slope_ref, up_ref, tokens_ref, share_ref, multiplier_ref, span_ref, hidden_ref
):
    @pl.when(pl.program_id(0) == 0)
    def _():
        hidden_ref[...] = jnp.concatenate(
            [grad_ref[y, :, start:end].astype(jnp.float32) for y, start, end in pieces], axis=1
        ).reshape(hidden_ref.shape)

    step = pl.program_id(0)
    tokens = tokens_ref[...].astype(jnp.float32)
    rows, width = tokens.shape
    count = IMAGE_BLOCK
    patches = rows // count
    hidden = hidden_ref.shape[2]
    grads = hidden_ref[step]
    slope = slope_ref[...].reshape(count, patches, hidden)
    preact_grad = (grads[:, None, :] * slope).astype(jnp.bfloat16).reshape(rows, hidden)
    normed = lax.dot_general(
        preact_grad, up_ref[...], (((1,), (1,)), ((), ())), preferred_element_type=jnp.float32
    )
    inner = norm_backward(tokens, normed, multiplier_ref[...])
    share = share_ref[step]
    span_ref[...] = (
        (share[:, None, :] + inner.reshape(count, patches, width))
        .astype(jnp.bfloat16)
        .reshape(rows, width)
    )


def span(received, pieces, slope, up_whole, tokens, share, multiplier):
    count, width = tokens.shape
    images = share.shape[0]
    share = share.reshape(images // IMAGE_BLOCK, IMAGE_BLOCK, width)
    hidden = slope.shape[1]
    rows = IMAGE_BLOCK * (count // images)
    whole = lambda array: pl.BlockSpec(array.shape, lambda i: (0,) * array.ndim)
    block = lambda columns: pl.BlockSpec((rows, columns), lambda i: (i, 0))
    return pl.pallas_call(
        functools.partial(span_kernel, pieces),
        grid=(count // rows,),
        in_specs=[
            whole(received),
            block(hidden),
            whole(up_whole),
            block(width),
            whole(share),
            whole(multiplier),
        ],
        out_specs=block(width),
        out_shape=jax.ShapeDtypeStruct((count, width), jnp.bfloat16),
        scratch_shapes=[pltpu.VMEM((images // IMAGE_BLOCK, IMAGE_BLOCK, hidden), jnp.float32)],
        compiler_params=pltpu.CompilerParams(vmem_limit_bytes=VMEM_BYTES),
        cost_estimate=pl.CostEstimate(
            flops=2 * count * hidden * width,
            bytes_accessed=4 * count * hidden + 2 * hidden * width + 4 * count * width,
            transcendentals=0,
        ),
    )(received, slope, up_whole, tokens, share, multiplier)


def exchange_y(blocks):
    return lax.all_to_all(blocks, "y", 0, 0)


def in_order_of_y(ahead, y):
    placed = [
        lax.select_n(y, *[ahead[(a - own) % Y_SHARDS] for own in range(Y_SHARDS)])
        for a in range(Y_SHARDS)
    ]
    return jnp.concatenate(placed, axis=0)


def per_device(
    feedforward_entry_states,
    stored_hidden_preacts,
    layernorm_multiplier,
    expanding_projector,
    contracting_projector,
    caption_tower_outputs,
    similarity_sharpness,
    similarity_shift_term,
    objective_upstream_grad,
):
    images, patches, model_width = feedforward_entry_states.shape[1:]
    hidden = stored_hidden_preacts.shape[-1]
    z, y = lax.axis_index("z"), lax.axis_index("y")
    z_size = lax.axis_size("z")
    shard_rows = contracting_projector.shape[1]
    shard_end = images + shard_rows
    block_rows = -(-shard_end // ROW_TILE) * ROW_TILE
    part = z_size * block_rows
    row = images * Y_SHARDS
    sharpness = similarity_sharpness[0]
    shift = similarity_shift_term[0]
    factor = objective_upstream_grad[0] * sharpness

    block = jnp.concatenate(
        [
            caption_tower_outputs[0],
            contracting_projector[0],
            jnp.zeros((block_rows - shard_end, model_width), jnp.bfloat16),
        ],
        axis=0,
    )
    blocks = lax.all_gather(block, "z", axis=0, tiled=True)

    tokens = feedforward_entry_states[0].reshape(images * patches, model_width).astype(jnp.float32)
    preact = stored_hidden_preacts[0].astype(jnp.float32)
    activated = jax.nn.gelu(preact, approximate=True).astype(jnp.bfloat16).astype(jnp.float32)
    mean_activated = jnp.mean(activated, axis=1)
    mean_tokens = jnp.mean(tokens.reshape(images, patches, model_width), axis=1)

    mean_sent = (
        jnp.pad(
            mean_activated.reshape(images, z_size, Y_SHARDS, shard_rows),
            ((0, 0), (0, 0), (0, 0), (images, block_rows - shard_end)),
        )
        .transpose(2, 0, 1, 3)
        .reshape(Y_SHARDS, images, part)
    )

    mean_sent, up_shard = lax.optimization_barrier((mean_sent, expanding_projector[0]))
    up_y = in_order_of_y(
        [up_shard] + [from_ahead(up_shard, "y", k) for k in range(1, Y_SHARDS)], y
    )
    up_whole = lax.all_gather(up_y, "z", axis=0, tiled=True)

    row_mean = exchange_y(mean_sent).reshape(row, part)
    own_means = jnp.where(
        jnp.arange(Y_SHARDS, dtype=jnp.int32)[:, None, None] == y, mean_tokens[None], 0.0
    ).reshape(row, model_width)
    shared = exchange_y(
        small_call(
            functools.partial(partial_kernel, images),
            (Y_SHARDS, row + z_size * images, model_width),
            (row_mean, blocks, own_means),
            4 * row * part * model_width,
        )
    )
    text_all = shared[:, row:].reshape(-1, model_width)
    pooled = jnp.sum(shared[:, :row].astype(jnp.float32), axis=0)
    image_dir, image_inverse = unit_rows(pooled)
    image_unit = image_dir.astype(jnp.bfloat16)

    def index_of(z_index, y_index):
        start = (z_index * Y_SHARDS + y_index) * images
        return start[..., None] + lax.iota(jnp.int32, images)

    def weigh(image_rows, image_index, text_rows, text_index):
        return pair_weights(
            image_rows, text_rows, image_index, text_index, sharpness, shift, factor
        )

    weights = weigh(
        image_unit,
        index_of(z, jnp.arange(Y_SHARDS, dtype=jnp.int32)).reshape(-1),
        text_all,
        index_of(
            lax.broadcasted_iota(jnp.int32, (Y_SHARDS, z_size), 1),
            lax.broadcasted_iota(jnp.int32, (Y_SHARDS, z_size), 0),
        ).reshape(-1),
    )
    image_sum = jnp.dot(weights, text_all, preferred_element_type=jnp.float32)
    pooled_grad = (
        image_sum - image_dir * jnp.sum(image_dir * image_sum, axis=-1, keepdims=True)
    ) * image_inverse
    row_share = pooled_grad / patches
    row_grad = row_share.astype(jnp.bfloat16)
    share = lax.dynamic_slice_in_dim(row_share, y * images, images, axis=0)
    preacts, row_grad = lax.optimization_barrier((stored_hidden_preacts[0], row_grad))
    slope = slopes(preacts.reshape(images * patches, hidden))
    sent_back = small_call(
        back_kernel, (row, part), (row_grad, blocks), 2 * row * part * model_width
    )
    received = exchange_y(sent_back.reshape(Y_SHARDS, images, part))
    column_sums = lax.dot_general(
        lax.dynamic_slice_in_dim(weights, y * z_size * images, z_size * images, axis=1),
        image_unit,
        (((0,), (0,)), ((), ())),
        preferred_element_type=jnp.float32,
    )
    pieces = [
        (
            own,
            at * block_rows + images,
            at * block_rows + shard_end,
        )
        for at in range(z_size)
        for own in range(Y_SHARDS)
    ]
    span_grad = span(
        received,
        pieces,
        slope,
        up_whole,
        feedforward_entry_states.reshape(images * patches, model_width),
        share,
        layernorm_multiplier,
    ).reshape(images, patches, model_width)
    column_sums, span_grad = lax.optimization_barrier(
        (column_sums.astype(jnp.bfloat16), span_grad)
    )
    prev_grad = from_ahead(span_grad[None], "section", 1)
    text_sums = lax.all_to_all(
        column_sums.reshape(z_size, images, model_width), "z", 0, 0
    )
    text_sums, prev_grad = lax.optimization_barrier((text_sums, prev_grad))
    text_sum = jnp.sum(text_sums.astype(jnp.float32), axis=0)

    text_dir, text_inverse = unit_rows(caption_tower_outputs[0].astype(jnp.float32))
    text_grad = (
        (text_sum - text_dir * jnp.sum(text_dir * text_sum, axis=-1, keepdims=True)) * text_inverse
    ).astype(jnp.bfloat16)
    return (prev_grad, text_grad[None])


def solution(mesh):
    sections, shards = mesh.devices.shape
    folded = Mesh(
        mesh.devices.reshape(sections, shards // Y_SHARDS, Y_SHARDS), ("section", "z", "y")
    )
    dp = ("z", "y")
    placed = (
        P("section", dp, None, None),
        P("section", dp, None, None),
        P("section", None),
        P("section", dp, None),
        P("section", dp, None),
        P("section", dp, None),
        P(),
        P(),
        P(),
    )
    return jax.shard_map(
        per_device,
        mesh=folded,
        in_specs=placed,
        out_specs=(P("section", dp, None, None), P("section", dp, None)),
        check_vma=False,
    )
```

```python
import functools

import jax
import jax.numpy as jnp
from jax import lax
from jax.experimental import pallas as pl
from jax.experimental.pallas import tpu as pltpu
from jax.sharding import Mesh, PartitionSpec as P

EPSILON = 1e-06
TANH_SCALE = 0.7978845608028654
CUBIC_TERM = 0.044715
Y_SHARDS = 4
ROW_TILE = 8
IMAGE_BLOCK = 8
VMEM_BYTES = 50 * 1024 * 1024


def from_ahead(array, axis, by):
    peers = lax.axis_size(axis)
    return lax.ppermute(array, axis, [((i + by) % peers, i) for i in range(peers)])


def gelu_slope(preact):
    inner = TANH_SCALE * (preact + CUBIC_TERM * preact * preact * preact)
    tangent = jnp.tanh(inner)
    return 0.5 * (1.0 + tangent) + 0.5 * preact * (1.0 - tangent * tangent) * TANH_SCALE * (
        1.0 + 3.0 * CUBIC_TERM * preact * preact
    )


def unit_rows(values):
    inverse = lax.rsqrt(jnp.sum(values * values, axis=-1, keepdims=True) + EPSILON)
    return (values * inverse, inverse)


def pair_weights(image_unit, text_unit, image_index, text_index, sharpness, shift, factor):
    logits = (
        sharpness
        * lax.dot_general(
            image_unit, text_unit, (((1,), (1,)), ((), ())), preferred_element_type=jnp.float32
        )
        + shift
    )
    signs = jnp.where(image_index[:, None] == text_index[None, :], 1.0, -1.0).astype(jnp.float32)
    return (factor * -signs * jax.nn.sigmoid(-signs * logits)).astype(jnp.bfloat16)


def norm_backward(tokens, normed_grad, layernorm_multiplier):
    centered = tokens - jnp.mean(tokens, axis=-1, keepdims=True)
    inverse = lax.rsqrt(jnp.mean(centered * centered, axis=-1, keepdims=True) + EPSILON)
    normal = centered * inverse
    scaled = normed_grad * layernorm_multiplier
    return inverse * (
        scaled
        - jnp.mean(scaled, axis=-1, keepdims=True)
        - normal * jnp.mean(scaled * normal, axis=-1, keepdims=True)
    )


def partial_kernel(images, means_ref, blocks_ref, own_ref, sent_ref):
    means = means_ref[...]
    high = means.astype(jnp.bfloat16)
    low = (means - high.astype(jnp.float32)).astype(jnp.bfloat16)
    blocks = blocks_ref[...]
    sums = jnp.dot(high, blocks, preferred_element_type=jnp.float32)
    sums = sums + jnp.dot(low, blocks, preferred_element_type=jnp.float32)
    sums = (sums + own_ref[...]).astype(jnp.bfloat16)
    rows, width = sums.shape
    blocks_z = sent_ref.shape[1] // images - rows // images
    block_rows = blocks.shape[0] // blocks_z
    for at in range(blocks_z):
        first = at * block_rows // 16 * 16
        skipped = at * block_rows - first
        last = -(-(skipped + images) // 16) * 16
        text = blocks_ref[first : first + last].astype(jnp.float32)[skipped : skipped + images]
        inverse = lax.rsqrt(jnp.sum(text * text, axis=-1, keepdims=True) + EPSILON)
        unit = (text * inverse).astype(jnp.bfloat16)
        for peer in range(sent_ref.shape[0]):
            sent_ref[peer, rows + at * images : rows + (at + 1) * images] = unit
    for peer in range(sent_ref.shape[0]):
        sent_ref[peer, :rows] = sums


def back_kernel(grads_ref, blocks_ref, sent_ref):
    hidden = lax.dot_general(
        grads_ref[...], blocks_ref[...], (((1,), (1,)), ((), ())), preferred_element_type=jnp.float32
    )
    sent_ref[...] = hidden.astype(jnp.bfloat16)


def small_call(kernel, shape, operands, flops):
    return pl.pallas_call(
        kernel,
        out_shape=jax.ShapeDtypeStruct(shape, jnp.bfloat16),
        in_specs=[pl.BlockSpec(memory_space=pltpu.VMEM)] * len(operands),
        out_specs=pl.BlockSpec(memory_space=pltpu.VMEM),
        compiler_params=pltpu.CompilerParams(vmem_limit_bytes=VMEM_BYTES),
        cost_estimate=pl.CostEstimate(flops=flops, bytes_accessed=2000000, transcendentals=0),
    )(*operands)


def slope_kernel(preact_ref, slope_ref):
    slope_ref[...] = gelu_slope(preact_ref[...].astype(jnp.float32))


def slopes(preact):
    tokens, hidden = preact.shape
    block = tokens // 4
    spec = pl.BlockSpec((block, hidden), lambda i: (i, 0))
    return pl.pallas_call(
        slope_kernel,
        grid=(tokens // block,),
        in_specs=[spec],
        out_specs=spec,
        out_shape=jax.ShapeDtypeStruct((tokens, hidden), jnp.float32),
        compiler_params=pltpu.CompilerParams(vmem_limit_bytes=VMEM_BYTES),
        cost_estimate=pl.CostEstimate(
            flops=20 * tokens * hidden, bytes_accessed=6 * tokens * hidden, transcendentals=0
        ),
    )(preact)


def span_kernel(
    pieces, grad_ref, slope_ref, up_ref, tokens_ref, share_ref, multiplier_ref, span_ref, hidden_ref
):
    @pl.when(pl.program_id(0) == 0)
    def _():
        hidden_ref[...] = jnp.concatenate(
            [grad_ref[y, :, start:end].astype(jnp.float32) for y, start, end in pieces], axis=1
        ).reshape(hidden_ref.shape)

    step = pl.program_id(0)
    tokens = tokens_ref[...].astype(jnp.float32)
    rows, width = tokens.shape
    count = IMAGE_BLOCK
    patches = rows // count
    hidden = hidden_ref.shape[2]
    grads = hidden_ref[step]
    slope = slope_ref[...].reshape(count, patches, hidden)
    preact_grad = (grads[:, None, :] * slope).astype(jnp.bfloat16).reshape(rows, hidden)
    normed = lax.dot_general(
        preact_grad, up_ref[...], (((1,), (1,)), ((), ())), preferred_element_type=jnp.float32
    )
    inner = norm_backward(tokens, normed, multiplier_ref[...])
    share = share_ref[step]
    span_ref[...] = (
        (share[:, None, :] + inner.reshape(count, patches, width))
        .astype(jnp.bfloat16)
        .reshape(rows, width)
    )


def span(received, pieces, slope, up_whole, tokens, share, multiplier):
    count, width = tokens.shape
    images = share.shape[0]
    share = share.reshape(images // IMAGE_BLOCK, IMAGE_BLOCK, width)
    hidden = slope.shape[1]
    rows = IMAGE_BLOCK * (count // images)
    whole = lambda array: pl.BlockSpec(array.shape, lambda i: (0,) * array.ndim)
    block = lambda columns: pl.BlockSpec((rows, columns), lambda i: (i, 0))
    return pl.pallas_call(
        functools.partial(span_kernel, pieces),
        grid=(count // rows,),
        in_specs=[
            whole(received),
            block(hidden),
            whole(up_whole),
            block(width),
            whole(share),
            whole(multiplier),
        ],
        out_specs=block(width),
        out_shape=jax.ShapeDtypeStruct((count, width), jnp.bfloat16),
        scratch_shapes=[pltpu.VMEM((images // IMAGE_BLOCK, IMAGE_BLOCK, hidden), jnp.float32)],
        compiler_params=pltpu.CompilerParams(vmem_limit_bytes=VMEM_BYTES),
        cost_estimate=pl.CostEstimate(
            flops=2 * count * hidden * width,
            bytes_accessed=4 * count * hidden + 2 * hidden * width + 4 * count * width,
            transcendentals=0,
        ),
    )(received, slope, up_whole, tokens, share, multiplier)


def exchange_y(blocks):
    return lax.all_to_all(blocks, "y", 0, 0)


def in_order_of_y(ahead, y):
    placed = [
        lax.select_n(y, *[ahead[(a - own) % Y_SHARDS] for own in range(Y_SHARDS)])
        for a in range(Y_SHARDS)
    ]
    return jnp.concatenate(placed, axis=0)


def per_device(
    feedforward_entry_states,
    stored_hidden_preacts,
    layernorm_multiplier,
    expanding_projector,
    contracting_projector,
    caption_tower_outputs,
    similarity_sharpness,
    similarity_shift_term,
    objective_upstream_grad,
):
    images, patches, model_width = feedforward_entry_states.shape[1:]
    hidden = stored_hidden_preacts.shape[-1]
    z, y = lax.axis_index("z"), lax.axis_index("y")
    z_size = lax.axis_size("z")
    shard_rows = contracting_projector.shape[1]
    shard_end = images + shard_rows
    block_rows = -(-shard_end // ROW_TILE) * ROW_TILE
    part = z_size * block_rows
    row = images * Y_SHARDS
    sharpness = similarity_sharpness[0]
    shift = similarity_shift_term[0]
    factor = objective_upstream_grad[0] * sharpness

    block = jnp.concatenate(
        [
            caption_tower_outputs[0],
            contracting_projector[0],
            jnp.zeros((block_rows - shard_end, model_width), jnp.bfloat16),
        ],
        axis=0,
    )
    blocks = lax.all_gather(block, "z", axis=0, tiled=True)

    tokens = feedforward_entry_states[0].reshape(images * patches, model_width).astype(jnp.float32)
    preact = stored_hidden_preacts[0].astype(jnp.float32)
    activated = jax.nn.gelu(preact, approximate=True).astype(jnp.bfloat16).astype(jnp.float32)
    mean_activated = jnp.mean(activated, axis=1)
    mean_tokens = jnp.mean(tokens.reshape(images, patches, model_width), axis=1)

    mean_sent = (
        jnp.pad(
            mean_activated.reshape(images, z_size, Y_SHARDS, shard_rows),
            ((0, 0), (0, 0), (0, 0), (images, block_rows - shard_end)),
        )
        .transpose(2, 0, 1, 3)
        .reshape(Y_SHARDS, images, part)
    )

    mean_sent, up_shard = lax.optimization_barrier((mean_sent, expanding_projector[0]))
    up_y = in_order_of_y(
        [up_shard] + [from_ahead(up_shard, "y", k) for k in range(1, Y_SHARDS)], y
    )
    up_whole = lax.all_gather(up_y, "z", axis=0, tiled=True)

    row_mean = exchange_y(mean_sent).reshape(row, part)
    own_means = jnp.where(
        jnp.arange(Y_SHARDS, dtype=jnp.int32)[:, None, None] == y, mean_tokens[None], 0.0
    ).reshape(row, model_width)
    shared = exchange_y(
        small_call(
            functools.partial(partial_kernel, images),
            (Y_SHARDS, row + z_size * images, model_width),
            (row_mean, blocks, own_means),
            4 * row * part * model_width,
        )
    )
    text_all = shared[:, row:].reshape(-1, model_width)
    pooled = jnp.sum(shared[:, :row].astype(jnp.float32), axis=0)
    image_dir, image_inverse = unit_rows(pooled)
    image_unit = image_dir.astype(jnp.bfloat16)

    def index_of(z_index, y_index):
        start = (z_index * Y_SHARDS + y_index) * images
        return start[..., None] + lax.iota(jnp.int32, images)

    def weigh(image_rows, image_index, text_rows, text_index):
        return pair_weights(
            image_rows, text_rows, image_index, text_index, sharpness, shift, factor
        )

    weights = weigh(
        image_unit,
        index_of(z, jnp.arange(Y_SHARDS, dtype=jnp.int32)).reshape(-1),
        text_all,
        index_of(
            lax.broadcasted_iota(jnp.int32, (Y_SHARDS, z_size), 1),
            lax.broadcasted_iota(jnp.int32, (Y_SHARDS, z_size), 0),
        ).reshape(-1),
    )
    image_sum = jnp.dot(weights, text_all, preferred_element_type=jnp.float32)
    pooled_grad = (
        image_sum - image_dir * jnp.sum(image_dir * image_sum, axis=-1, keepdims=True)
    ) * image_inverse
    row_share = pooled_grad / patches
    row_grad = row_share.astype(jnp.bfloat16)
    share = lax.dynamic_slice_in_dim(row_share, y * images, images, axis=0)
    preacts, row_grad = lax.optimization_barrier((stored_hidden_preacts[0], row_grad))
    slope = slopes(preacts.reshape(images * patches, hidden))
    sent_back = small_call(
        back_kernel, (row, part), (row_grad, blocks), 2 * row * part * model_width
    )
    received = exchange_y(sent_back.reshape(Y_SHARDS, images, part))
    column_sums = lax.dot_general(
        lax.dynamic_slice_in_dim(weights, y * z_size * images, z_size * images, axis=1),
        image_unit,
        (((0,), (0,)), ((), ())),
        preferred_element_type=jnp.float32,
    )
    pieces = [
        (
            own,
            at * block_rows + images,
            at * block_rows + shard_end,
        )
        for at in range(z_size)
        for own in range(Y_SHARDS)
    ]
    span_grad = span(
        received,
        pieces,
        slope,
        up_whole,
        feedforward_entry_states.reshape(images * patches, model_width),
        share,
        layernorm_multiplier,
    ).reshape(images, patches, model_width)
    column_sums, span_grad = lax.optimization_barrier(
        (column_sums.astype(jnp.bfloat16), span_grad)
    )
    prev_grad = from_ahead(span_grad[None], "section", 1)
    text_sums = lax.all_to_all(
        column_sums.reshape(z_size, images, model_width), "z", 0, 0
    )
    text_sums, prev_grad = lax.optimization_barrier((text_sums, prev_grad))
    text_sum = jnp.sum(text_sums.astype(jnp.float32), axis=0)

    text_dir, text_inverse = unit_rows(caption_tower_outputs[0].astype(jnp.float32))
    text_grad = (
        (text_sum - text_dir * jnp.sum(text_dir * text_sum, axis=-1, keepdims=True)) * text_inverse
    ).astype(jnp.bfloat16)
    return (prev_grad, text_grad[None])


def solution(mesh):
    sections, shards = mesh.devices.shape
    folded = Mesh(
        mesh.devices.reshape(sections, shards // Y_SHARDS, Y_SHARDS), ("section", "z", "y")
    )
    dp = ("z", "y")
    placed = (
        P("section", dp, None, None),
        P("section", dp, None, None),
        P("section", None),
        P("section", dp, None),
        P("section", dp, None),
        P("section", dp, None),
        P(),
        P(),
        P(),
    )
    return jax.shard_map(
        per_device,
        mesh=folded,
        in_specs=placed,
        out_specs=(P("section", dp, None, None), P("section", dp, None)),
        check_vma=False,
    )
```

```python
import functools

import jax
import jax.numpy as jnp
from jax import lax
from jax.experimental import pallas as pl
from jax.experimental.pallas import tpu as pltpu
from jax.sharding import Mesh, PartitionSpec as P

EPSILON = 1e-06
TANH_SCALE = 0.7978845608028654
CUBIC_TERM = 0.044715
Y_SHARDS = 4
ROW_TILE = 8
IMAGE_BLOCK = 8
VMEM_BYTES = 50 * 1024 * 1024


def from_ahead(array, axis, by):
    peers = lax.axis_size(axis)
    return lax.ppermute(array, axis, [((i + by) % peers, i) for i in range(peers)])


def gelu_slope(preact):
    inner = TANH_SCALE * (preact + CUBIC_TERM * preact * preact * preact)
    tangent = jnp.tanh(inner)
    return 0.5 * (1.0 + tangent) + 0.5 * preact * (1.0 - tangent * tangent) * TANH_SCALE * (
        1.0 + 3.0 * CUBIC_TERM * preact * preact
    )


def unit_rows(values):
    inverse = lax.rsqrt(jnp.sum(values * values, axis=-1, keepdims=True) + EPSILON)
    return (values * inverse, inverse)


def pair_weights(image_unit, text_unit, image_index, text_index, sharpness, shift, factor):
    logits = (
        sharpness
        * lax.dot_general(
            image_unit, text_unit, (((1,), (1,)), ((), ())), preferred_element_type=jnp.float32
        )
        + shift
    )
    signs = jnp.where(image_index[:, None] == text_index[None, :], 1.0, -1.0).astype(jnp.float32)
    return (factor * -signs * jax.nn.sigmoid(-signs * logits)).astype(jnp.bfloat16)


def norm_backward(tokens, normed_grad, layernorm_multiplier):
    centered = tokens - jnp.mean(tokens, axis=-1, keepdims=True)
    inverse = lax.rsqrt(jnp.mean(centered * centered, axis=-1, keepdims=True) + EPSILON)
    normal = centered * inverse
    scaled = normed_grad * layernorm_multiplier
    return inverse * (
        scaled
        - jnp.mean(scaled, axis=-1, keepdims=True)
        - normal * jnp.mean(scaled * normal, axis=-1, keepdims=True)
    )


def partial_kernel(images, means_ref, blocks_ref, own_ref, sent_ref):
    means = means_ref[...]
    high = means.astype(jnp.bfloat16)
    low = (means - high.astype(jnp.float32)).astype(jnp.bfloat16)
    blocks = blocks_ref[...]
    sums = jnp.dot(high, blocks, preferred_element_type=jnp.float32)
    sums = sums + jnp.dot(low, blocks, preferred_element_type=jnp.float32)
    sums = (sums + own_ref[...]).astype(jnp.bfloat16)
    rows, width = sums.shape
    blocks_z = sent_ref.shape[1] // images - rows // images
    block_rows = blocks.shape[0] // blocks_z
    for at in range(blocks_z):
        first = at * block_rows // 16 * 16
        skipped = at * block_rows - first
        last = -(-(skipped + images) // 16) * 16
        text = blocks_ref[first : first + last].astype(jnp.float32)[skipped : skipped + images]
        inverse = lax.rsqrt(jnp.sum(text * text, axis=-1, keepdims=True) + EPSILON)
        unit = (text * inverse).astype(jnp.bfloat16)
        for peer in range(sent_ref.shape[0]):
            sent_ref[peer, rows + at * images : rows + (at + 1) * images] = unit
    for peer in range(sent_ref.shape[0]):
        sent_ref[peer, :rows] = sums


def back_kernel(grads_ref, blocks_ref, sent_ref):
    hidden = lax.dot_general(
        grads_ref[...], blocks_ref[...], (((1,), (1,)), ((), ())), preferred_element_type=jnp.float32
    )
    sent_ref[...] = hidden.astype(jnp.bfloat16)


def small_call(kernel, shape, operands, flops):
    return pl.pallas_call(
        kernel,
        out_shape=jax.ShapeDtypeStruct(shape, jnp.bfloat16),
        in_specs=[pl.BlockSpec(memory_space=pltpu.VMEM)] * len(operands),
        out_specs=pl.BlockSpec(memory_space=pltpu.VMEM),
        compiler_params=pltpu.CompilerParams(vmem_limit_bytes=VMEM_BYTES),
        cost_estimate=pl.CostEstimate(flops=flops, bytes_accessed=2000000, transcendentals=0),
    )(*operands)


def slope_kernel(preact_ref, slope_ref):
    slope_ref[...] = gelu_slope(preact_ref[...].astype(jnp.float32))


def slopes(preact):
    tokens, hidden = preact.shape
    block = tokens // 4
    spec = pl.BlockSpec((block, hidden), lambda i: (i, 0))
    return pl.pallas_call(
        slope_kernel,
        grid=(tokens // block,),
        in_specs=[spec],
        out_specs=spec,
        out_shape=jax.ShapeDtypeStruct((tokens, hidden), jnp.float32),
        compiler_params=pltpu.CompilerParams(vmem_limit_bytes=VMEM_BYTES),
        cost_estimate=pl.CostEstimate(
            flops=20 * tokens * hidden, bytes_accessed=6 * tokens * hidden, transcendentals=0
        ),
    )(preact)


def preact_kernel(pieces, grad_ref, slope_ref, preact_grad_ref, hidden_ref):
    step = pl.program_id(0)

    @pl.when(step == 0)
    def _():
        hidden_ref[...] = jnp.concatenate(
            [grad_ref[y, :, start:end].astype(jnp.float32) for y, start, end in pieces], axis=1
        ).reshape(hidden_ref.shape)

    rows = preact_grad_ref.shape[0]
    _, count, hidden = hidden_ref.shape
    slope = slope_ref[...].reshape(count, rows // count, hidden)
    preact_grad_ref[...] = (
        (hidden_ref[step][:, None, :] * slope).astype(jnp.bfloat16).reshape(rows, hidden)
    )


def preact_grads(received, pieces, slope, images):
    count, hidden = slope.shape
    rows = IMAGE_BLOCK * (count // images)
    block = pl.BlockSpec((rows, hidden), lambda i: (i, 0))
    return pl.pallas_call(
        functools.partial(preact_kernel, pieces),
        grid=(count // rows,),
        in_specs=[pl.BlockSpec(received.shape, lambda i: (0, 0, 0)), block],
        out_specs=block,
        out_shape=jax.ShapeDtypeStruct((count, hidden), jnp.bfloat16),
        scratch_shapes=[pltpu.VMEM((images // IMAGE_BLOCK, IMAGE_BLOCK, hidden), jnp.float32)],
        compiler_params=pltpu.CompilerParams(vmem_limit_bytes=VMEM_BYTES),
        cost_estimate=pl.CostEstimate(
            flops=2 * count * hidden, bytes_accessed=6 * count * hidden, transcendentals=0
        ),
    )(received, slope)


def span_kernel(grads_ref, up_ref, tokens_ref, share_ref, multiplier_ref, span_ref):
    tokens = tokens_ref[...].astype(jnp.float32)
    rows, width = tokens.shape
    patches = rows // IMAGE_BLOCK
    normed = lax.dot_general(
        grads_ref[...], up_ref[...], (((1,), (1,)), ((), ())), preferred_element_type=jnp.float32
    )
    inner = norm_backward(tokens, normed, multiplier_ref[...])
    share = share_ref[pl.program_id(0)]
    span_ref[...] = (
        (share[:, None, :] + inner.reshape(IMAGE_BLOCK, patches, width))
        .astype(jnp.bfloat16)
        .reshape(rows, width)
    )


def span(preact_grad, up_whole, tokens, share, multiplier):
    count, width = tokens.shape
    images = share.shape[0]
    share = share.reshape(images // IMAGE_BLOCK, IMAGE_BLOCK, width)
    hidden = preact_grad.shape[1]
    rows = IMAGE_BLOCK * (count // images)
    whole = lambda array: pl.BlockSpec(array.shape, lambda i: (0,) * array.ndim)
    block = lambda columns: pl.BlockSpec((rows, columns), lambda i: (i, 0))
    return pl.pallas_call(
        span_kernel,
        grid=(count // rows,),
        in_specs=[
            block(hidden),
            whole(up_whole),
            block(width),
            whole(share),
            whole(multiplier),
        ],
        out_specs=block(width),
        out_shape=jax.ShapeDtypeStruct((count, width), jnp.bfloat16),
        compiler_params=pltpu.CompilerParams(vmem_limit_bytes=VMEM_BYTES),
        cost_estimate=pl.CostEstimate(
            flops=2 * count * hidden * width,
            bytes_accessed=2 * count * hidden + 2 * hidden * width + 4 * count * width,
            transcendentals=0,
        ),
    )(preact_grad, up_whole, tokens, share, multiplier)


def exchange_y(blocks):
    return lax.all_to_all(blocks, "y", 0, 0)


def in_order_of_y(ahead, y):
    placed = [
        lax.select_n(y, *[ahead[(a - own) % Y_SHARDS] for own in range(Y_SHARDS)])
        for a in range(Y_SHARDS)
    ]
    return jnp.concatenate(placed, axis=0)


def per_device(
    feedforward_entry_states,
    stored_hidden_preacts,
    layernorm_multiplier,
    expanding_projector,
    contracting_projector,
    caption_tower_outputs,
    similarity_sharpness,
    similarity_shift_term,
    objective_upstream_grad,
):
    images, patches, model_width = feedforward_entry_states.shape[1:]
    hidden = stored_hidden_preacts.shape[-1]
    z, y = lax.axis_index("z"), lax.axis_index("y")
    z_size = lax.axis_size("z")
    shard_rows = contracting_projector.shape[1]
    shard_end = images + shard_rows
    block_rows = -(-shard_end // ROW_TILE) * ROW_TILE
    part = z_size * block_rows
    row = images * Y_SHARDS
    sharpness = similarity_sharpness[0]
    shift = similarity_shift_term[0]
    factor = objective_upstream_grad[0] * sharpness

    block = jnp.concatenate(
        [
            caption_tower_outputs[0],
            contracting_projector[0],
            jnp.zeros((block_rows - shard_end, model_width), jnp.bfloat16),
        ],
        axis=0,
    )
    blocks = lax.all_gather(block, "z", axis=0, tiled=True)

    tokens = feedforward_entry_states[0].reshape(images * patches, model_width).astype(jnp.float32)
    preact = stored_hidden_preacts[0].astype(jnp.float32)
    activated = jax.nn.gelu(preact, approximate=True).astype(jnp.bfloat16).astype(jnp.float32)
    mean_activated = jnp.mean(activated, axis=1)
    mean_tokens = jnp.mean(tokens.reshape(images, patches, model_width), axis=1)

    mean_sent = (
        jnp.pad(
            mean_activated.reshape(images, z_size, Y_SHARDS, shard_rows),
            ((0, 0), (0, 0), (0, 0), (images, block_rows - shard_end)),
        )
        .transpose(2, 0, 1, 3)
        .reshape(Y_SHARDS, images, part)
    )

    mean_sent, up_shard = lax.optimization_barrier((mean_sent, expanding_projector[0]))
    up_y = in_order_of_y(
        [up_shard] + [from_ahead(up_shard, "y", k) for k in range(1, Y_SHARDS)], y
    )
    up_whole = lax.all_gather(up_y, "z", axis=0, tiled=True)

    row_mean = exchange_y(mean_sent).reshape(row, part)
    own_means = jnp.where(
        jnp.arange(Y_SHARDS, dtype=jnp.int32)[:, None, None] == y, mean_tokens[None], 0.0
    ).reshape(row, model_width)
    shared = exchange_y(
        small_call(
            functools.partial(partial_kernel, images),
            (Y_SHARDS, row + z_size * images, model_width),
            (row_mean, blocks, own_means),
            4 * row * part * model_width,
        )
    )
    text_all = shared[:, row:].reshape(-1, model_width)
    pooled = jnp.sum(shared[:, :row].astype(jnp.float32), axis=0)
    image_dir, image_inverse = unit_rows(pooled)
    image_unit = image_dir.astype(jnp.bfloat16)

    def index_of(z_index, y_index):
        start = (z_index * Y_SHARDS + y_index) * images
        return start[..., None] + lax.iota(jnp.int32, images)

    def weigh(image_rows, image_index, text_rows, text_index):
        return pair_weights(
            image_rows, text_rows, image_index, text_index, sharpness, shift, factor
        )

    weights = weigh(
        image_unit,
        index_of(z, jnp.arange(Y_SHARDS, dtype=jnp.int32)).reshape(-1),
        text_all,
        index_of(
            lax.broadcasted_iota(jnp.int32, (Y_SHARDS, z_size), 1),
            lax.broadcasted_iota(jnp.int32, (Y_SHARDS, z_size), 0),
        ).reshape(-1),
    )
    image_sum = jnp.dot(weights, text_all, preferred_element_type=jnp.float32)
    pooled_grad = (
        image_sum - image_dir * jnp.sum(image_dir * image_sum, axis=-1, keepdims=True)
    ) * image_inverse
    row_share = pooled_grad / patches
    row_grad = row_share.astype(jnp.bfloat16)
    share = lax.dynamic_slice_in_dim(row_share, y * images, images, axis=0)
    preacts, row_grad = lax.optimization_barrier((stored_hidden_preacts[0], row_grad))
    slope = slopes(preacts.reshape(images * patches, hidden))
    sent_back = small_call(
        back_kernel, (row, part), (row_grad, blocks), 2 * row * part * model_width
    )
    received = exchange_y(sent_back.reshape(Y_SHARDS, images, part))
    column_sums = lax.dot_general(
        lax.dynamic_slice_in_dim(weights, y * z_size * images, z_size * images, axis=1),
        image_unit,
        (((0,), (0,)), ((), ())),
        preferred_element_type=jnp.float32,
    )
    pieces = [
        (
            own,
            at * block_rows + images,
            at * block_rows + shard_end,
        )
        for at in range(z_size)
        for own in range(Y_SHARDS)
    ]
    span_grad = span(
        preact_grads(received, pieces, slope, images),
        up_whole,
        feedforward_entry_states.reshape(images * patches, model_width),
        share,
        layernorm_multiplier,
    ).reshape(images, patches, model_width)
    column_sums, span_grad = lax.optimization_barrier(
        (column_sums.astype(jnp.bfloat16), span_grad)
    )
    prev_grad = from_ahead(span_grad[None], "section", 1)
    text_sums = lax.all_to_all(
        column_sums.reshape(z_size, images, model_width), "z", 0, 0
    )
    text_sums, prev_grad = lax.optimization_barrier((text_sums, prev_grad))
    text_sum = jnp.sum(text_sums.astype(jnp.float32), axis=0)

    text_dir, text_inverse = unit_rows(caption_tower_outputs[0].astype(jnp.float32))
    text_grad = (
        (text_sum - text_dir * jnp.sum(text_dir * text_sum, axis=-1, keepdims=True)) * text_inverse
    ).astype(jnp.bfloat16)
    return (prev_grad, text_grad[None])


def solution(mesh):
    sections, shards = mesh.devices.shape
    folded = Mesh(
        mesh.devices.reshape(sections, shards // Y_SHARDS, Y_SHARDS), ("section", "z", "y")
    )
    dp = ("z", "y")
    placed = (
        P("section", dp, None, None),
        P("section", dp, None, None),
        P("section", None),
        P("section", dp, None),
        P("section", dp, None),
        P("section", dp, None),
        P(),
        P(),
        P(),
    )
    return jax.shard_map(
        per_device,
        mesh=folded,
        in_specs=placed,
        out_specs=(P("section", dp, None, None), P("section", dp, None)),
        check_vma=False,
    )
```

```python
import functools

import jax
import jax.numpy as jnp
from jax import lax
from jax.experimental import pallas as pl
from jax.experimental.pallas import tpu as pltpu
from jax.sharding import Mesh, PartitionSpec as P

EPSILON = 1e-06
TANH_SCALE = 0.7978845608028654
CUBIC_TERM = 0.044715
Y_SHARDS = 4
ROW_TILE = 8
IMAGE_BLOCK = 8
VMEM_BYTES = 50 * 1024 * 1024


def from_ahead(array, axis, by):
    peers = lax.axis_size(axis)
    return lax.ppermute(array, axis, [((i + by) % peers, i) for i in range(peers)])


def gelu_slope(preact):
    inner = TANH_SCALE * (preact + CUBIC_TERM * preact * preact * preact)
    tangent = jnp.tanh(inner)
    return 0.5 * (1.0 + tangent) + 0.5 * preact * (1.0 - tangent * tangent) * TANH_SCALE * (
        1.0 + 3.0 * CUBIC_TERM * preact * preact
    )


def unit_rows(values):
    inverse = lax.rsqrt(jnp.sum(values * values, axis=-1, keepdims=True) + EPSILON)
    return (values * inverse, inverse)


def pair_weights(image_unit, text_unit, image_index, text_index, sharpness, shift, factor):
    logits = (
        sharpness
        * lax.dot_general(
            image_unit, text_unit, (((1,), (1,)), ((), ())), preferred_element_type=jnp.float32
        )
        + shift
    )
    signs = jnp.where(image_index[:, None] == text_index[None, :], 1.0, -1.0).astype(jnp.float32)
    return (factor * -signs * jax.nn.sigmoid(-signs * logits)).astype(jnp.bfloat16)


def norm_backward(tokens, normed_grad, layernorm_multiplier):
    centered = tokens - jnp.mean(tokens, axis=-1, keepdims=True)
    inverse = lax.rsqrt(jnp.mean(centered * centered, axis=-1, keepdims=True) + EPSILON)
    scaled = normed_grad * layernorm_multiplier
    along = jnp.mean(scaled * centered, axis=-1, keepdims=True) * inverse * inverse
    return inverse * (scaled - jnp.mean(scaled, axis=-1, keepdims=True) - centered * along)


def partial_kernel(images, means_ref, blocks_ref, own_ref, sent_ref):
    means = means_ref[...]
    high = means.astype(jnp.bfloat16)
    low = (means - high.astype(jnp.float32)).astype(jnp.bfloat16)
    blocks = blocks_ref[...]
    sums = jnp.dot(high, blocks, preferred_element_type=jnp.float32)
    sums = sums + jnp.dot(low, blocks, preferred_element_type=jnp.float32)
    sums = (sums + own_ref[...]).astype(jnp.bfloat16)
    rows, width = sums.shape
    blocks_z = sent_ref.shape[1] // images - rows // images
    block_rows = blocks.shape[0] // blocks_z
    for at in range(blocks_z):
        first = at * block_rows // 16 * 16
        skipped = at * block_rows - first
        last = -(-(skipped + images) // 16) * 16
        text = blocks_ref[first : first + last].astype(jnp.float32)[skipped : skipped + images]
        inverse = lax.rsqrt(jnp.sum(text * text, axis=-1, keepdims=True) + EPSILON)
        unit = (text * inverse).astype(jnp.bfloat16)
        for peer in range(sent_ref.shape[0]):
            sent_ref[peer, rows + at * images : rows + (at + 1) * images] = unit
    for peer in range(sent_ref.shape[0]):
        sent_ref[peer, :rows] = sums


def back_kernel(grads_ref, blocks_ref, sent_ref):
    hidden = lax.dot_general(
        grads_ref[...], blocks_ref[...], (((1,), (1,)), ((), ())), preferred_element_type=jnp.float32
    )
    sent_ref[...] = hidden.astype(jnp.bfloat16)


def small_call(kernel, shape, operands, flops):
    return pl.pallas_call(
        kernel,
        out_shape=jax.ShapeDtypeStruct(shape, jnp.bfloat16),
        in_specs=[pl.BlockSpec(memory_space=pltpu.VMEM)] * len(operands),
        out_specs=pl.BlockSpec(memory_space=pltpu.VMEM),
        compiler_params=pltpu.CompilerParams(vmem_limit_bytes=VMEM_BYTES),
        cost_estimate=pl.CostEstimate(flops=flops, bytes_accessed=2000000, transcendentals=0),
    )(*operands)


def slope_kernel(preact_ref, slope_ref):
    slope_ref[...] = gelu_slope(preact_ref[...].astype(jnp.float32)).astype(jnp.bfloat16)


def slopes(preact):
    tokens, hidden = preact.shape
    block = tokens // 4
    spec = pl.BlockSpec((block, hidden), lambda i: (i, 0))
    return pl.pallas_call(
        slope_kernel,
        grid=(tokens // block,),
        in_specs=[spec],
        out_specs=spec,
        out_shape=jax.ShapeDtypeStruct((tokens, hidden), jnp.bfloat16),
        compiler_params=pltpu.CompilerParams(vmem_limit_bytes=VMEM_BYTES),
        cost_estimate=pl.CostEstimate(
            flops=20 * tokens * hidden, bytes_accessed=4 * tokens * hidden, transcendentals=0
        ),
    )(preact)


def span_kernel(
    pieces, grad_ref, slope_ref, up_ref, tokens_ref, share_ref, multiplier_ref, span_ref, hidden_ref
):
    @pl.when(pl.program_id(0) == 0)
    def _():
        hidden_ref[...] = jnp.concatenate(
            [grad_ref[y, :, start:end].astype(jnp.float32) for y, start, end in pieces], axis=1
        ).reshape(hidden_ref.shape)

    step = pl.program_id(0)
    tokens = tokens_ref[...].astype(jnp.float32)
    rows, width = tokens.shape
    count = IMAGE_BLOCK
    patches = rows // count
    hidden = hidden_ref.shape[2]
    grads = hidden_ref[step]
    slope = slope_ref[...].astype(jnp.float32).reshape(count, patches, hidden)
    preact_grad = (grads[:, None, :] * slope).astype(jnp.bfloat16).reshape(rows, hidden)
    normed = lax.dot_general(
        preact_grad, up_ref[...], (((1,), (1,)), ((), ())), preferred_element_type=jnp.float32
    )
    inner = norm_backward(tokens, normed, multiplier_ref[...])
    share = share_ref[step]
    span_ref[...] = (
        (share[:, None, :] + inner.reshape(count, patches, width))
        .astype(jnp.bfloat16)
        .reshape(rows, width)
    )


def span(received, pieces, slope, up_whole, tokens, share, multiplier):
    count, width = tokens.shape
    images = share.shape[0]
    share = share.reshape(images // IMAGE_BLOCK, IMAGE_BLOCK, width)
    hidden = slope.shape[1]
    rows = IMAGE_BLOCK * (count // images)
    whole = lambda array: pl.BlockSpec(array.shape, lambda i: (0,) * array.ndim)
    block = lambda columns: pl.BlockSpec((rows, columns), lambda i: (i, 0))
    return pl.pallas_call(
        functools.partial(span_kernel, pieces),
        grid=(count // rows,),
        in_specs=[
            whole(received),
            block(hidden),
            whole(up_whole),
            block(width),
            whole(share),
            whole(multiplier),
        ],
        out_specs=block(width),
        out_shape=jax.ShapeDtypeStruct((count, width), jnp.bfloat16),
        scratch_shapes=[pltpu.VMEM((images // IMAGE_BLOCK, IMAGE_BLOCK, hidden), jnp.float32)],
        compiler_params=pltpu.CompilerParams(vmem_limit_bytes=VMEM_BYTES),
        cost_estimate=pl.CostEstimate(
            flops=2 * count * hidden * width,
            bytes_accessed=4 * count * hidden + 2 * hidden * width + 4 * count * width,
            transcendentals=0,
        ),
    )(received, slope, up_whole, tokens, share, multiplier)


def exchange_y(blocks):
    return lax.all_to_all(blocks, "y", 0, 0)


def in_order_of_y(ahead, y):
    placed = [
        lax.select_n(y, *[ahead[(a - own) % Y_SHARDS] for own in range(Y_SHARDS)])
        for a in range(Y_SHARDS)
    ]
    return jnp.concatenate(placed, axis=0)


def per_device(
    feedforward_entry_states,
    stored_hidden_preacts,
    layernorm_multiplier,
    expanding_projector,
    contracting_projector,
    caption_tower_outputs,
    similarity_sharpness,
    similarity_shift_term,
    objective_upstream_grad,
):
    images, patches, model_width = feedforward_entry_states.shape[1:]
    hidden = stored_hidden_preacts.shape[-1]
    z, y = lax.axis_index("z"), lax.axis_index("y")
    z_size = lax.axis_size("z")
    shard_rows = contracting_projector.shape[1]
    shard_end = images + shard_rows
    block_rows = -(-shard_end // ROW_TILE) * ROW_TILE
    part = z_size * block_rows
    row = images * Y_SHARDS
    sharpness = similarity_sharpness[0]
    shift = similarity_shift_term[0]
    factor = objective_upstream_grad[0] * sharpness

    block = jnp.concatenate(
        [
            caption_tower_outputs[0],
            contracting_projector[0],
            jnp.zeros((block_rows - shard_end, model_width), jnp.bfloat16),
        ],
        axis=0,
    )
    blocks = lax.all_gather(block, "z", axis=0, tiled=True)

    tokens = feedforward_entry_states[0].reshape(images * patches, model_width).astype(jnp.float32)
    preact = stored_hidden_preacts[0].astype(jnp.float32)
    activated = jax.nn.gelu(preact, approximate=True).astype(jnp.bfloat16).astype(jnp.float32)
    mean_activated = jnp.mean(activated, axis=1)
    mean_tokens = jnp.mean(tokens.reshape(images, patches, model_width), axis=1)

    mean_sent = (
        jnp.pad(
            mean_activated.reshape(images, z_size, Y_SHARDS, shard_rows),
            ((0, 0), (0, 0), (0, 0), (images, block_rows - shard_end)),
        )
        .transpose(2, 0, 1, 3)
        .reshape(Y_SHARDS, images, part)
    )

    mean_sent, up_shard = lax.optimization_barrier((mean_sent, expanding_projector[0]))
    up_y = in_order_of_y(
        [up_shard] + [from_ahead(up_shard, "y", k) for k in range(1, Y_SHARDS)], y
    )
    up_whole = lax.all_gather(up_y, "z", axis=0, tiled=True)

    row_mean = exchange_y(mean_sent).reshape(row, part)
    own_means = jnp.where(
        jnp.arange(Y_SHARDS, dtype=jnp.int32)[:, None, None] == y, mean_tokens[None], 0.0
    ).reshape(row, model_width)
    shared = exchange_y(
        small_call(
            functools.partial(partial_kernel, images),
            (Y_SHARDS, row + z_size * images, model_width),
            (row_mean, blocks, own_means),
            4 * row * part * model_width,
        )
    )
    text_all = shared[:, row:].reshape(-1, model_width)
    pooled = jnp.sum(shared[:, :row].astype(jnp.float32), axis=0)
    image_dir, image_inverse = unit_rows(pooled)
    image_unit = image_dir.astype(jnp.bfloat16)

    def index_of(z_index, y_index):
        start = (z_index * Y_SHARDS + y_index) * images
        return start[..., None] + lax.iota(jnp.int32, images)

    def weigh(image_rows, image_index, text_rows, text_index):
        return pair_weights(
            image_rows, text_rows, image_index, text_index, sharpness, shift, factor
        )

    weights = weigh(
        image_unit,
        index_of(z, jnp.arange(Y_SHARDS, dtype=jnp.int32)).reshape(-1),
        text_all,
        index_of(
            lax.broadcasted_iota(jnp.int32, (Y_SHARDS, z_size), 1),
            lax.broadcasted_iota(jnp.int32, (Y_SHARDS, z_size), 0),
        ).reshape(-1),
    )
    image_sum = jnp.dot(weights, text_all, preferred_element_type=jnp.float32)
    pooled_grad = (
        image_sum - image_dir * jnp.sum(image_dir * image_sum, axis=-1, keepdims=True)
    ) * image_inverse
    row_share = pooled_grad / patches
    row_grad = row_share.astype(jnp.bfloat16)
    share = lax.dynamic_slice_in_dim(row_share, y * images, images, axis=0)
    preacts, row_grad = lax.optimization_barrier((stored_hidden_preacts[0], row_grad))
    slope = slopes(preacts.reshape(images * patches, hidden))
    sent_back = small_call(
        back_kernel, (row, part), (row_grad, blocks), 2 * row * part * model_width
    )
    received = exchange_y(sent_back.reshape(Y_SHARDS, images, part))
    column_sums = lax.dot_general(
        lax.dynamic_slice_in_dim(weights, y * z_size * images, z_size * images, axis=1),
        image_unit,
        (((0,), (0,)), ((), ())),
        preferred_element_type=jnp.float32,
    )
    pieces = [
        (
            own,
            at * block_rows + images,
            at * block_rows + shard_end,
        )
        for at in range(z_size)
        for own in range(Y_SHARDS)
    ]
    span_grad = span(
        received,
        pieces,
        slope,
        up_whole,
        feedforward_entry_states.reshape(images * patches, model_width),
        share,
        layernorm_multiplier,
    ).reshape(images, patches, model_width)
    column_sums, span_grad = lax.optimization_barrier(
        (column_sums.astype(jnp.bfloat16), span_grad)
    )
    prev_grad = from_ahead(span_grad[None], "section", 1)
    text_sums = lax.all_to_all(
        column_sums.reshape(z_size, images, model_width), "z", 0, 0
    )
    text_sums, prev_grad = lax.optimization_barrier((text_sums, prev_grad))
    text_sum = jnp.sum(text_sums.astype(jnp.float32), axis=0)

    text_dir, text_inverse = unit_rows(caption_tower_outputs[0].astype(jnp.float32))
    text_grad = (
        (text_sum - text_dir * jnp.sum(text_dir * text_sum, axis=-1, keepdims=True)) * text_inverse
    ).astype(jnp.bfloat16)
    return (prev_grad, text_grad[None])


def solution(mesh):
    sections, shards = mesh.devices.shape
    folded = Mesh(
        mesh.devices.reshape(sections, shards // Y_SHARDS, Y_SHARDS), ("section", "z", "y")
    )
    dp = ("z", "y")
    placed = (
        P("section", dp, None, None),
        P("section", dp, None, None),
        P("section", None),
        P("section", dp, None),
        P("section", dp, None),
        P("section", dp, None),
        P(),
        P(),
        P(),
    )
    return jax.shard_map(
        per_device,
        mesh=folded,
        in_specs=placed,
        out_specs=(P("section", dp, None, None), P("section", dp, None)),
        check_vma=False,
    )
```
